32 devices in a mesh: leaf: 2 (over y), frow: 4 (over z), fcol: 4 (over x, core).
Axes of the slice: x: 2, y: 2, z: 4, core: 2. Of those that a mesh axis runs over, the one named last changes fastest.
Arguments:
- child_fronts: float32 [2, 4096, 4096], P('leaf', 'frow', 'fcol'), may hold values from -20 to 120, as said below
- parent_front: float32 [4096, 4096], P('frow', 'fcol'), may hold values from -20 to 120, as said below
- block_maps: int32 [2, 32], P('leaf'), may hold values from 0 to 31, as said below
Outputs:
- child_factors: float32 [2, 4096, 4096], P('leaf', 'frow', 'fcol')
- parent_factor: float32 [4096, 4096], P('frow', 'fcol')
The draws below stay inside these ranges and needn't reach their ends.
Inputs may be any that keep to these rules, and one draw needn't show every extreme that they name: Each row block_maps[l] is a permutation of the block numbers that keeps every block inside its group of 8 consecutive blocks: block_maps[l, i] // 8 == i // 8. `child_fronts`: every child front is symmetric positive definite. `parent_front`: the parent front is symmetric positive definite.
All inputs are finite; a program needn't handle non-finite values.
Results may differ from the reference program's by a relative error of at most 0.0001.
Values sent between devices are 32-bit elements; how exact they have to be, the bound alone decides.
A program may use at most 64 MiB of HBM per device.

```python
import math
import jax
import jax.numpy as jnp
from jax import lax

BLOCK = 128
FRONT = 4096
CHILD_PANELS = 2
PARENT_PANELS = 1
CHILDREN = 2
BLOCKS = 32
GROUP = 8


common_rank = 256


common_weight = 2.0


def symmetric_base(key, members, lowest, highest):
    noise_key = jax.random.fold_in(key, 31)
    diagonal_key = jax.random.fold_in(key, 37)
    common_key = jax.random.fold_in(key, 43)
    half_width = 0.5 * math.sqrt(3.0 / FRONT)
    uniform_noise = jax.random.uniform(noise_key, (members, FRONT, FRONT), jnp.float32, -half_width, half_width)
    symmetric = (uniform_noise + jnp.swapaxes(uniform_noise, 1, 2)) * 0.5
    factors = jax.random.uniform(common_key, (members, FRONT, common_rank), jnp.float32, -math.sqrt(3.0), math.sqrt(3.0))
    shared = jnp.einsum('mik,mjk->mij', factors, factors, precision=lax.Precision.HIGHEST) * (common_weight / common_rank)
    shared = (shared + jnp.swapaxes(shared, 1, 2)) * 0.5
    diagonal = jax.random.uniform(diagonal_key, (members, FRONT), jnp.float32, lowest, highest)
    identity = jnp.eye(FRONT, dtype=jnp.float32)
    return symmetric + shared + diagonal[:, :, None] * identity[None, :, :]


def draw_child_fronts(key, part):
    matrix = symmetric_base(jax.random.fold_in(key, 11), CHILDREN, 2.0, 4.0)
    return matrix


def draw_parent_front(key, part):
    matrix = symmetric_base(jax.random.fold_in(key, 21), 1, 1.0, 2.0)
    return matrix[0]


def draw_block_maps(key, part):
    scores = jax.random.randint(jax.random.fold_in(key, 41), (CHILDREN, BLOCKS), 0, 4096)
    slot_index = jnp.arange(BLOCKS, dtype=jnp.int32)
    grouped = slot_index // GROUP * (4096 * BLOCKS) + scores * BLOCKS + slot_index[None, :]
    return jnp.argsort(grouped, axis=1).astype(jnp.int32)


def setup_inputs(seed: int = 0) -> dict:
    keys = jax.random.split(jax.random.key(seed), 4)
    return {
        "child_fronts": draw_child_fronts(jax.random.fold_in(keys[3], 71), 0),
        "parent_front": draw_parent_front(jax.random.fold_in(keys[3], 71), 0),
        "block_maps": draw_block_maps(jax.random.fold_in(keys[3], 71), 0),
    }


def partial_factor(matrix, panels):
    for number in range(panels):
        first_col = number * BLOCK
        end_col = first_col + BLOCK
        factor = jnp.linalg.cholesky(matrix[first_col:end_col, first_col:end_col])
        lower_rows = lax.linalg.triangular_solve(factor, matrix[end_col:, first_col:end_col], left_side=False, lower=True, transpose_a=True)
        column = jnp.concatenate([jnp.zeros((first_col, BLOCK), jnp.float32), factor, lower_rows], axis=0)
        matrix = matrix.at[:, first_col:end_col].set(column)
        matrix = matrix.at[first_col:end_col, end_col:].set(0.0)
        matrix = matrix.at[end_col:, end_col:].add(-jnp.dot(lower_rows, lower_rows.T, precision=lax.Precision.HIGHEST))
    return matrix

def reference(child_fronts, parent_front, block_maps):
    positions = jnp.arange(FRONT, dtype=jnp.int32)
    trailing = positions >= CHILD_PANELS * BLOCK
    assembled = parent_front
    factored = []
    for child_index in range(CHILDREN):
        finished = partial_factor(child_fronts[child_index], CHILD_PANELS)
        factored.append(finished)
        target = (block_maps[child_index][positions // BLOCK] * BLOCK + positions % BLOCK).astype(jnp.int32)
        contribution = jnp.where(trailing[:, None] & trailing[None, :], finished, 0.0)
        assembled = assembled.at[target[:, None], target[None, :]].add(contribution)
    return (jnp.stack(factored), partial_factor(assembled, PARENT_PANELS))
```

```python
import functools

import jax
import jax.numpy as jnp
from jax import lax
from jax.experimental import pallas as pl
from jax.experimental.pallas import tpu as pltpu
from jax.sharding import PartitionSpec as P

BLOCK = 128
CHILD_PANELS = 2
WIDE = BLOCK * CHILD_PANELS
HIGHEST = lax.Precision.HIGHEST


def dot(a, b, contract=((1,), (0,))):
    return lax.dot_general(
        a, b, (contract, ((), ())), precision=HIGHEST, preferred_element_type=jnp.float32
    )


def factor_block(matrix):
    groups = BLOCK // 8
    sub = lax.broadcasted_iota(jnp.int32, (8, BLOCK), 0)
    lane = lax.broadcasted_iota(jnp.int32, (8, BLOCK), 1)
    rows = [matrix[g * 8 : g * 8 + 8, :] for g in range(groups)]
    inverse = [jnp.where(lane == sub + g * 8, 1.0, 0.0) for g in range(groups)]
    for k in range(BLOCK):
        own, within = divmod(k, 8)
        pivot_row = rows[own][within : within + 1, :]
        scale = 1.0 / pivot_row[:, k : k + 1]
        pivot_row = pivot_row * scale
        inverse_row = inverse[own][within : within + 1, :] * scale
        for g in range(own, groups):
            if g == own and within == 7:
                continue
            column = rows[g][:, k : k + 1]
            if g == own:
                column = jnp.where(sub[:, :1] > within, column, 0.0)
            rows[g] = rows[g] - column * pivot_row
            inverse[g] = inverse[g] - column * inverse_row
    upper, lower_inverse = [], []
    for g in range(groups):
        diagonal = jnp.sum(jnp.where(lane == sub + g * 8, rows[g], 0.0), axis=1, keepdims=True)
        root = 1.0 / jnp.sqrt(diagonal)
        upper.append(jnp.where(lane >= sub + g * 8, rows[g] * root, 0.0))
        lower_inverse.append(inverse[g] * root)
    return jnp.concatenate(upper, axis=0), jnp.concatenate(lower_inverse, axis=0)


def factor_kernel(panels, d_ref, k_ref, w_ref):
    k_ref[...] = jnp.zeros_like(k_ref)
    w_ref[...] = jnp.zeros_like(w_ref)
    for p in range(panels):
        c = slice(p * BLOCK, (p + 1) * BLOCK)
        block = d_ref[c, c]
        if p:
            before = slice(0, p * BLOCK)
            left = dot(d_ref[c, before], w_ref[before, before], ((1,), (1,)))
            k_ref[c, before] = left
            block = block - dot(left, left, ((1,), (1,)))
        upper, inverse = factor_block(block)
        k_ref[c, c] = upper.T
        w_ref[c, c] = inverse
        if p:
            w_ref[c, before] = -dot(inverse, dot(left, w_ref[before, before]))


def factor(pivot):
    size = pivot.shape[0]
    shape = jax.ShapeDtypeStruct((size, size), jnp.float32)
    return pl.pallas_call(
        functools.partial(factor_kernel, size // BLOCK),
        out_shape=(shape, shape),
        in_specs=[pl.BlockSpec(memory_space=pltpu.VMEM)],
        out_specs=(pl.BlockSpec(memory_space=pltpu.VMEM),) * 2,
        cost_estimate=pl.CostEstimate(
            flops=size * BLOCK * 2000, bytes_accessed=3 * size * size * 4, transcendentals=0
        ),
        name="factor_pivot",
    )(pivot)


def parent_kernel(children, tables, where_am_i, *refs):
    front, panel_rows, panel_cols, pivot_factor = refs[:4]
    blocks = refs[4 : 4 + children]
    left = refs[4 + children : 4 + 2 * children]
    right = refs[4 + 2 * children : 4 + 3 * children]
    out, held = refs[4 + 3 * children], refs[5 + 3 * children]
    r = pl.program_id(0)
    row_blocks = pl.num_programs(0)
    col_blocks = out.shape[1] // BLOCK
    for s in range(children):
        held[s] = blocks[s][...] - dot(left[s][...], right[s][...])
    update = dot(panel_rows[...], panel_cols[...])
    first_row = (where_am_i[0] == 0) & (r == 0)
    for c in range(col_blocks):
        cols = slice(c * BLOCK, (c + 1) * BLOCK)
        tile = front[:, cols]
        for s in range(children):
            source = tables[s, 2, c]
            keep = tables[s, 1, r] * tables[s, 3, c]
            piece = held[s, :, pl.ds(pl.multiple_of(source * BLOCK, BLOCK), BLOCK)]
            tile = tile + jnp.where(keep > 0, piece, 0.0)
        tile = tile - update[:, cols]
        tile = jnp.where(first_row, 0.0, tile)
        if c == 0:
            pivot = jnp.where(first_row, pivot_factor[...], panel_rows[...])
            tile = jnp.where(where_am_i[1] == 0, pivot, tile)
        out[:, cols] = tile


def finish_parent(tables, where_am_i, front, panel_rows, panel_cols, pivot_factor, blocks, left, right):
    height, breadth = front.shape
    children = len(blocks)

    def moved(s):
        return lambda r, tables, where_am_i: (tables[s, 0, r], 0)

    def row(r, tables, where_am_i):
        return (r, 0)

    def whole(r, tables, where_am_i):
        return (0, 0)

    return pl.pallas_call(
        functools.partial(parent_kernel, children),
        grid_spec=pltpu.PrefetchScalarGridSpec(
            num_scalar_prefetch=2,
            grid=(height // BLOCK,),
            in_specs=[
                pl.BlockSpec((BLOCK, breadth), row),
                pl.BlockSpec((BLOCK, BLOCK), row),
                pl.BlockSpec((BLOCK, breadth), whole),
                pl.BlockSpec((BLOCK, BLOCK), whole),
            ]
            + [pl.BlockSpec((BLOCK, breadth), moved(s)) for s in range(children)]
            + [pl.BlockSpec((BLOCK, WIDE), moved(s)) for s in range(children)]
            + [pl.BlockSpec((WIDE, breadth), whole) for s in range(children)],
            out_specs=pl.BlockSpec((BLOCK, breadth), row),
            scratch_shapes=[pltpu.VMEM((children, BLOCK, breadth), jnp.float32)],
        ),
        out_shape=jax.ShapeDtypeStruct((height, breadth), jnp.float32),
        compiler_params=pltpu.CompilerParams(
            dimension_semantics=("arbitrary",), vmem_limit_bytes=40 * 2**20
        ),
        cost_estimate=pl.CostEstimate(
            flops=2 * height * breadth * (WIDE * children + BLOCK) * 6,
            bytes_accessed=height * breadth * 4 * (children + 2),
            transcendentals=0,
        ),
        name="finish_parent",
    )(tables, where_am_i, front, panel_rows, panel_cols, pivot_factor, *blocks, *left, *right)


def moved_blocks(array, source, kept, axis):
    pieces = []
    for place in range(array.shape[axis] // BLOCK):
        piece = lax.dynamic_slice_in_dim(array, source[place] * BLOCK, BLOCK, axis)
        pieces.append(jnp.where(kept[place] > 0, piece, 0.0))
    return jnp.concatenate(pieces, axis)


def per_device(leaves, frows, fcols, child_fronts, parent_front, block_maps):
    own = child_fronts[0]
    height, breadth = own.shape
    row_blocks, col_blocks = height // BLOCK, breadth // BLOCK
    l, i, j = lax.axis_index("leaf"), lax.axis_index("frow"), lax.axis_index("fcol")
    axes = ("leaf", "frow", "fcol")

    def send(x, moves):
        flat = lambda c: (c[0] * frows + c[1]) * fcols + c[2]
        return lax.ppermute(x, axes, [(flat(a), flat(b)) for a, b in moves])

    def along_row(x):
        step = fcols // 2
        while step:
            sources = range(0, fcols, 2 * step)
            moves = [
                ((a, b, c), (a, b, c + step))
                for a in range(leaves) for b in range(frows) for c in sources
            ]
            x = jnp.where(lax.rem(j, 2 * step) == step, send(x, moves), x)
            step //= 2
        return x

    def along_col(x, columns):
        for b in range(frows - 1):
            moves = [((a, b, c), (a, b + 1, c)) for a in range(leaves) for c in columns]
            x = jnp.where(i == b + 1, send(x, moves), x)
        return x

    def from_leaf(x, shift, rows=range(frows), columns=range(fcols)):
        return send(
            x,
            [((a, b, c), ((a + shift) % leaves, b, c)) for a in range(leaves) for b in rows for c in columns],
        )

    number = jnp.arange(block_maps.shape[1], dtype=jnp.int32)
    maps = [block_maps[0]] + [lax.ppermute(block_maps[0], "leaf", [(a, (a + s) % leaves) for a in range(leaves)]) for s in range(1, leaves)]
    inverses = [jnp.sum(jnp.where(m[:, None] == number[None, :], number[:, None], 0), axis=0) for m in maps]
    width = max(row_blocks, col_blocks)
    tables = []
    for inverse in inverses:
        mine_rows = lax.dynamic_slice_in_dim(inverse, i * row_blocks, row_blocks)
        mine_cols = lax.dynamic_slice_in_dim(inverse, j * col_blocks, col_blocks)
        lines = [
            mine_rows - i * row_blocks,
            (mine_rows >= CHILD_PANELS).astype(jnp.int32),
            mine_cols - j * col_blocks,
            (mine_cols >= CHILD_PANELS).astype(jnp.int32),
        ]
        tables.append(jnp.stack([jnp.pad(line, (0, width - line.shape[0])) for line in lines]))
    tables = jnp.stack(tables)
    first = [inverse[0] for inverse in inverses]

    own_rows = jnp.concatenate(
        [own[:, :WIDE], lax.dynamic_slice(own, (0, first[0] * BLOCK), (height, BLOCK))], axis=1
    )
    own_cols = jnp.concatenate(
        [own[:WIDE], lax.dynamic_slice(own, (first[0] * BLOCK, 0), (BLOCK, breadth))], axis=0
    )
    raw_rows = [own_rows] + [from_leaf(own_rows, s, columns=(0,)) for s in range(1, leaves)]
    raw_cols = [own_cols] + [from_leaf(own_cols, s, rows=(0,)) for s in range(1, leaves)]
    blocks = [own] + [from_leaf(own, s) for s in range(1, leaves)]

    left, right, factors = [], [], []
    for s in range(leaves):
        pivot = along_col(raw_rows[s][:WIDE, :WIDE], (0,))
        message = along_row(jnp.concatenate([pivot, raw_rows[s][:, :WIDE]], axis=0))
        cols = along_col(raw_cols[s][:WIDE], range(fcols))
        k, w = factor(message[:WIDE])
        factors.append(k)
        left.append(dot(message[WIDE:], w, ((1,), (1,))))
        right.append(dot(w, cols))

    global_rows = i * height + jnp.arange(height, dtype=jnp.int32)[:, None]
    global_cols = j * breadth + jnp.arange(breadth, dtype=jnp.int32)[None, :]
    trailing = (global_rows >= WIDE) & (global_cols >= WIDE)
    finished = jnp.where(trailing, own - dot(left[0], right[0]), 0.0)
    panel = jnp.concatenate([jnp.where(i == 0, factors[0], left[0][:WIDE]), left[0][WIDE:]], axis=0)
    finished = finished.at[:, :WIDE].set(jnp.where(j == 0, panel, finished[:, :WIDE]))

    panel_rows, panel_cols = parent_front[:, :BLOCK], parent_front[:BLOCK]
    for s in range(leaves):
        across = lax.dynamic_slice(right[s], (0, first[s] * BLOCK), (WIDE, BLOCK))
        part = raw_rows[s][:, WIDE:] - dot(left[s], across)
        part = moved_blocks(part, tables[s, 0], tables[s, 1], 0)
        panel_rows = panel_rows + jnp.where(first[s] >= CHILD_PANELS, part, 0.0)
        down = lax.dynamic_slice(left[s], (first[s] * BLOCK, 0), (BLOCK, WIDE))
        part = raw_cols[s][WIDE:] - dot(down, right[s])
        part = moved_blocks(part, tables[s, 2], tables[s, 3], 1)
        panel_cols = panel_cols + jnp.where(first[s] >= CHILD_PANELS, part, 0.0)
    pivot = along_col(panel_rows[:BLOCK], (0,))
    message = along_row(jnp.concatenate([pivot, panel_rows], axis=0))
    panel_cols = along_col(panel_cols, range(fcols))
    k, w = factor(message[:BLOCK])
    panel_rows = dot(message[BLOCK:], w, ((1,), (1,)))
    panel_cols = dot(w, panel_cols)

    where_am_i = jnp.stack([i, j]).astype(jnp.int32)
    parent = finish_parent(
        tables, where_am_i, parent_front, panel_rows, panel_cols, k, blocks, left, right
    )
    return (finished[None], parent)


def solution(mesh):
    return jax.shard_map(
        functools.partial(per_device, mesh.shape["leaf"], mesh.shape["frow"], mesh.shape["fcol"]),
        mesh=mesh,
        in_specs=(P("leaf", "frow", "fcol"), P("frow", "fcol"), P("leaf", None)),
        out_specs=(P("leaf", "frow", "fcol"), P("frow", "fcol")),
        check_vma=False,
    )
```

```python
import functools

import jax
import jax.numpy as jnp
from jax import lax
from jax.experimental import pallas as pl
from jax.experimental.pallas import tpu as pltpu
from jax.sharding import PartitionSpec as P

BLOCK = 128
CHILD_PANELS = 2
WIDE = BLOCK * CHILD_PANELS
CHUNKS = 4
MESH = pl.DeviceIdType.MESH


def dot(a, b, contract=((1,), (0,))):
    return lax.dot_general(
        a, b, (contract, ((), ())),
        precision=lax.Precision.HIGHEST, preferred_element_type=jnp.float32,
    )


def dot_t(a, b):
    return dot(a, b, ((1,), (1,)))


def factor_block(block, between):
    shape = (BLOCK, BLOCK)
    row = lax.broadcasted_iota(jnp.int32, shape, 0)
    lane = lax.broadcasted_iota(jnp.int32, shape, 1)

    def turn(g, carry):
        m, v = carry
        active = row < BLOCK - 8 * g
        for t in range(8):
            scale = 1.0 / m[t : t + 1, t : t + 1]
            column = jnp.where(active & (row > t), jnp.broadcast_to(m[:, t : t + 1], shape), 0.0)
            pivot_m = m[t : t + 1, :] * scale
            pivot_v = v[t : t + 1, :] * scale
            m = m - column * pivot_m
            v = v - column * pivot_v
        m = pltpu.roll(m, BLOCK - 8, 1)
        m = jnp.concatenate([m[8:], m[:8]], axis=0)
        v = jnp.concatenate([v[8:], v[:8]], axis=0)
        return m, v

    carry = (block, jnp.where(row == lane, 1.0, 0.0))
    half = BLOCK // 16
    carry = lax.fori_loop(0, half, turn, carry)
    between()
    m, v = lax.fori_loop(half, 2 * half, turn, carry)
    between()
    root = 1.0 / jnp.sqrt(jnp.sum(jnp.where(row == lane, m, 0.0), axis=1, keepdims=True))
    return jnp.where(lane >= row, m * root, 0.0), v * root


def kernel(sizes, table, table_send, own, front, child, other, update, tables,
           stage, dbuf, piv, rows, cols, left, right, corr, kbuf, wbuf,
           prow, pcol, ppiv, down_part, across, kp, lprow, lpcol, send_sem, recv_sem):
    leaves, frows, fcols = sizes
    height, breadth = own.shape
    rb, cb = height // BLOCK, breadth // BLOCK
    has_c = rb > CHILD_PANELS and cb > CHILD_PANELS
    l, i, j = lax.axis_index("leaf"), lax.axis_index("frow"), lax.axis_index("fcol")
    top, first = i == 0, j == 0
    corner = top & first
    pending = []
    names = {}

    def sem(*name):
        return recv_sem.at[names.setdefault(name, len(names))]

    def start(cond, src, dst, signal, where):
        copy = pltpu.make_async_remote_copy(
            src_ref=src, dst_ref=dst, send_sem=send_sem.at[len(pending)], recv_sem=signal,
            device_id=where, device_id_type=MESH,
        )
        pending.append((cond, copy))
        pl.when(cond)(copy.start)

    def arrived(cond, dst, signal, where):
        copy = pltpu.make_async_remote_copy(
            src_ref=dst, dst_ref=dst, send_sem=send_sem.at[0], recv_sem=signal,
            device_id=where, device_id_type=MESH,
        )
        pl.when(cond)(copy.wait_recv)

    always = i >= 0
    up = {"frow": lax.rem(i + 1, frows)}
    down = {"frow": lax.rem(i + frows - 1, frows)}
    root_row = {"fcol": lax.rem(j + 1, fcols)}

    def leaf_at(s):
        return {"leaf": lax.rem(l + s, leaves)}

    def rows_of(k):
        return pl.ds(pl.multiple_of(k * BLOCK, BLOCK), BLOCK)

    def chunk(ref, q, count):
        size = ref.shape[0] // count
        return ref.at[pl.ds(q * size, size)]

    barrier = pltpu.get_barrier_semaphore()
    for d in range(1, leaves):
        pl.semaphore_signal(barrier, inc=1, device_id=leaf_at(d), device_id_type=MESH)
    for d in range(1, frows):
        pl.semaphore_signal(barrier, inc=1, device_id={"frow": lax.rem(i + d, frows)}, device_id_type=MESH)
    for d in range(1, fcols):
        pl.semaphore_signal(barrier, inc=1, device_id={"fcol": lax.rem(j + d, fcols)}, device_id_type=MESH)
    pl.semaphore_wait(barrier, leaves + frows + fcols - 3)

    pivot_own = own.at[pl.ds(0, WIDE), pl.ds(0, WIDE)]

    def pivot_of(s):
        return pivot_own if s == 0 else other.at[s - 1, pl.ds(0, WIDE), pl.ds(0, WIDE)]

    def send_pivot(s):
        for b in range(1, frows):
            start(corner, pivot_of(s), dbuf.at[s], sem("d", s), {"frow": b})
        for c in range(1, fcols):
            if c % leaves == s:
                start(corner, pivot_of(s), piv, sem("piv"), {"fcol": c})

    def pass_pivot(s):
        inner = first & (i > 0)
        arrived(inner, dbuf.at[s], sem("d", s), down)
        for c in range(1, fcols):
            if c % leaves == s:
                start(inner, dbuf.at[s], piv, sem("piv"), {"fcol": c})

    send_pivot(0)
    for q in range(CHUNKS):
        start(top, chunk(own.at[pl.ds(0, WIDE)], q, CHUNKS), chunk(cols.at[0], q, CHUNKS), sem("c", 0, q), up)
    for c in range(1, fcols):
        start(first, own.at[:, pl.ds(0, WIDE)], rows.at[0], sem("r", 0), {"fcol": c})

    def is_at(ref, kind, k, t, shape):
        return jnp.broadcast_to(ref[kind, pl.ds(k, 1), 0:1], shape) == t

    def chosen(ref, kind, k, count, block):
        total = 0.0
        for t in range(count):
            part = block(t)
            total = total + jnp.where(is_at(ref, kind, k, t, part.shape), part, 0.0)
        return total

    def stage_rows(r, carry):
        stage[rows_of(r), :] = own[rows_of(r), :]
        return carry

    def block_slice(t):
        return slice(t * BLOCK, (t + 1) * BLOCK)

    def stage_cols(r, carry):
        held = stage[rows_of(r), block_slice(CHILD_PANELS)]
        value = held
        for t in range(CHILD_PANELS + 1, cb):
            here = stage[rows_of(r), block_slice(t)]
            match = is_at(table, 1, 0, t, here.shape)
            value = jnp.where(match, here, value)
            stage[rows_of(r), block_slice(t)] = jnp.where(match, held, here)
        stage[rows_of(r), block_slice(CHILD_PANELS)] = value
        return carry

    pieces = [(0, WIDE, 0, WIDE), (0, WIDE, WIDE, breadth)]
    early, late = 2, []
    if height > WIDE:
        three = WIDE + BLOCK
        pieces += [(WIDE, three, 0, breadth)]
        if height > three:
            pieces += [(three, height, 0, three), (three, height, three, breadth)]

    def piece(ref, n):
        a, b, c, d = pieces[n]
        return ref.at[pl.ds(a, b - a), pl.ds(c, d - c)]

    def send_pieces(numbers):
        for n in numbers:
            for s in range(1, leaves):
                start(always, piece(stage, n), piece(other.at[s - 1], n), sem("y", s, n), leaf_at(s))

    def wait_pieces(numbers):
        for n in numbers:
            for s in range(1, leaves):
                arrived(always, piece(other.at[s - 1], n), sem("y", s, n), leaf_at(leaves - s))

    for s in range(1, leaves):
        start(always, table_send, tables.at[s - 1], sem("tables", s), leaf_at(s))
    lax.fori_loop(0, CHILD_PANELS, stage_rows, 0)
    if has_c:
        @pl.when(first)
        def _():
            lax.fori_loop(0, CHILD_PANELS, stage_cols, 0)
    send_pieces(range(2))
    lax.fori_loop(CHILD_PANELS, rb, stage_rows, 0)
    if has_c:
        @pl.when(top)
        def _():
            def fix(c, carry):
                held = own[block_slice(CHILD_PANELS), rows_of(c)]
                value = held
                for t in range(CHILD_PANELS + 1, rb):
                    here = own[block_slice(t), rows_of(c)]
                    match = is_at(table, 0, 0, t, here.shape)
                    value = jnp.where(match, here, value)
                    stage[block_slice(t), rows_of(c)] = jnp.where(match, held, here)
                stage[block_slice(CHILD_PANELS), rows_of(c)] = value
                return carry

            lax.fori_loop(0, cb, fix, 0)

        @pl.when(first)
        def _():
            lax.fori_loop(CHILD_PANELS, rb, stage_cols, 0)
    send_pieces(range(2, len(pieces)))
    middle = list(range(2, min(4, len(pieces))))
    last = list(range(4, len(pieces)))

    @pl.when(top)
    def _():
        cols[0] = own[0:WIDE, :]

    @pl.when(first)
    def _():
        rows[0] = own[:, 0:WIDE]

    pass_pivot(0)

    @pl.when(corner)
    def _():
        piv[...] = own[0:WIDE, 0:WIDE]

    @pl.when(first & (i > 0))
    def _():
        piv[...] = dbuf[0]

    def pass_cols(s, q):
        here = chunk(cols.at[s], q, CHUNKS)
        arrived(i > 0, here, sem("c", s, q), down)
        start((i > 0) & (i < frows - 1), here, here, sem("c", s, q), up)

    for q in range(CHUNKS):
        pass_cols(0, q)

    wait_pieces(range(2))
    for s in range(1, leaves):
        send_pivot(s)
    for s in range(1, leaves):
        for q in range(CHUNKS):
            source = chunk(other.at[s - 1, pl.ds(0, WIDE)], q, CHUNKS)
            start(top, source, chunk(cols.at[s], q, CHUNKS), sem("c", s, q), up)
        pass_pivot(s)

        @pl.when(top)
        def _(s=s):
            cols[s] = other[s - 1, 0:WIDE, :]

    arrived(j > 0, piv, sem("piv"), root_row)
    slot = lax.rem(j, leaves)
    base = j - slot
    step = []

    def between():
        q = len(step)
        step.append(q)
        for s in range(1, leaves):
            pass_cols(s, q)
        if q == 1:
            wait_pieces(middle)
            for s in range(1, leaves):
                @pl.when(first)
                def _(s=s):
                    rows[s] = other[s - 1, :, 0:WIDE]

                for c in range(1, fcols):
                    start(first, other.at[s - 1, :, pl.ds(0, WIDE)], rows.at[s], sem("r", s), {"fcol": c})

    lo, hi = slice(0, BLOCK), slice(BLOCK, WIDE)
    upper, inverse = factor_block(piv[lo, lo], between)
    kbuf[...] = jnp.zeros_like(kbuf)
    kbuf[lo, lo] = upper.T
    wbuf[slot, lo, lo] = inverse
    wbuf[slot, lo, hi] = jnp.zeros((BLOCK, BLOCK), jnp.float32)
    below = dot_t(piv[hi, lo], inverse)
    kbuf[hi, lo] = below
    upper, second = factor_block(piv[hi, hi] - dot_t(below, below), between)
    kbuf[hi, hi] = upper.T
    wbuf[slot, hi, hi] = second
    wbuf[slot, hi, lo] = -dot(second, dot(below, inverse))
    w_sems = [sem("w", s) for s in range(leaves)]
    w_first = names[("w", 0)]
    for d in range(1, leaves):
        start(always, wbuf.at[slot], wbuf.at[slot], recv_sem.at[w_first + slot], {"fcol": base + lax.rem(slot + d, leaves)})
    for d in range(1, leaves):
        from_slot = lax.rem(slot + d, leaves)
        arrived(always, wbuf.at[from_slot], recv_sem.at[w_first + from_slot], {"fcol": base + from_slot})

    for s in range(1, leaves):
        arrived(always, tables.at[s - 1], sem("tables", s), leaf_at(leaves - s))

    def make_panels(s):
        if s:
            arrived(j > 0, rows.at[s], sem("r", s), root_row)

        def one_row(r, carry):
            left[s, rows_of(r), :] = dot_t(rows[s, rows_of(r), :], wbuf[s])
            return carry

        def one_col(c, carry):
            right[s, :, rows_of(c)] = dot(wbuf[s], cols[s, :, rows_of(c)])
            return carry

        lax.fori_loop(0, rb, one_row, 0)
        lax.fori_loop(0, cb, one_col, 0)

    arrived(j > 0, rows.at[0], sem("r", 0), root_row)
    for s in range(leaves):
        make_panels(s)

    third = block_slice(CHILD_PANELS)
    known = [table] + [tables.at[s - 1] for s in range(1, leaves)]

    @pl.when(first)
    def _():
        for s in range(leaves if has_c else 0):
            if s == 0:
                beside = chosen(table, 1, 0, cb, lambda t: right[0, :, block_slice(t)])
            else:
                beside = right[s, :, third]
                beside = jnp.where(is_at(known[s], 1, 0, CHILD_PANELS, beside.shape), beside, 0.0)

            def one(r, carry, s=s, beside=beside):
                if s == 0:
                    raw = chosen(table, 1, 0, cb, lambda t: own[rows_of(r), block_slice(t)])
                else:
                    raw = other[s - 1, rows_of(r), third]
                    raw = jnp.where(is_at(known[s], 1, 0, CHILD_PANELS, raw.shape), raw, 0.0)
                down_part[s, rows_of(r), :] = raw - dot(left[s, rows_of(r), :], beside)
                return carry

            lax.fori_loop(0, rb, one, 0)

        def assemble(r, carry):
            tile = front[rows_of(r), 0:BLOCK]
            for s in range(leaves if has_c else 0):
                tile = tile + chosen(known[s], 0, r, rb, lambda t: down_part[s, block_slice(t), :])
            prow[rows_of(r), :] = tile
            return carry

        lax.fori_loop(0, rb, assemble, 0)

    @pl.when(top)
    def _():
        for s in range(leaves if has_c else 0):
            if s == 0:
                beside = chosen(table, 0, 0, rb, lambda t: left[0, block_slice(t), :])
            else:
                beside = left[s, third, :]
                beside = jnp.where(is_at(known[s], 0, 0, CHILD_PANELS, beside.shape), beside, 0.0)

            def one(c, carry, s=s, beside=beside):
                if s == 0:
                    raw = chosen(table, 0, 0, rb, lambda t: own[block_slice(t), rows_of(c)])
                else:
                    raw = other[s - 1, third, rows_of(c)]
                    raw = jnp.where(is_at(known[s], 0, 0, CHILD_PANELS, raw.shape), raw, 0.0)
                across[s, :, rows_of(c)] = raw - dot(beside, right[s, :, rows_of(c)])
                return carry

            lax.fori_loop(0, cb, one, 0)

        def assemble(c, carry):
            tile = front[0:BLOCK, rows_of(c)]
            for s in range(leaves if has_c else 0):
                tile = tile + chosen(known[s], 1, c, cb, lambda t: across[s, :, block_slice(t)])
            pcol[:, rows_of(c)] = tile
            return carry

        lax.fori_loop(0, cb, assemble, 0)

    @pl.when(corner)
    def _():
        ppiv[...] = prow[0:BLOCK, :]

    for b in range(1, frows):
        start(corner, ppiv, ppiv, sem("pp"), {"frow": b})
    for c in range(1, fcols):
        start(corner, ppiv, ppiv, sem("pp"), {"fcol": c})
    for q in range(2):
        start(top, chunk(pcol, q, 2), chunk(pcol, q, 2), sem("pc", q), up)
    for c in range(1, fcols):
        start(first, prow, prow, sem("pr"), {"fcol": c})
    arrived(first & (i > 0), ppiv, sem("pp"), down)
    for c in range(1, fcols):
        start(first & (i > 0), ppiv, ppiv, sem("pp"), {"fcol": c})

    def child_row(r, carry):
        value = own[rows_of(r), :] - dot(left[0, rows_of(r), :], right[0])
        child[rows_of(r), :] = jnp.where(top & (r < CHILD_PANELS), 0.0, value)
        return carry

    lax.fori_loop(0, rb, child_row, 0)

    @pl.when(first)
    def _():
        child[:, 0:WIDE] = left[0]

    @pl.when(corner)
    def _():
        child[0:WIDE, 0:WIDE] = kbuf[...]

    arrived(j > 0, ppiv, sem("pp"), root_row)
    turn = []

    def pass_parent():
        q = len(turn)
        turn.append(q)
        part = chunk(pcol, q, 2)
        arrived(i > 0, part, sem("pc", q), down)
        start((i > 0) & (i < frows - 1), part, part, sem("pc", q), up)

    upper, inverse = factor_block(ppiv[...], pass_parent)
    kp[...] = upper.T
    for s in range(1, leaves):
        def corr_row(r, carry, s=s):
            corr[s - 1, rows_of(r), :] = dot(left[s, rows_of(r), :], right[s])
            return carry

        lax.fori_loop(0, rb, corr_row, 0)
    arrived(j > 0, prow, sem("pr"), root_row)
    lprow[...] = dot_t(prow[...], inverse)
    lpcol[...] = dot(inverse, pcol[...])

    def parent_row(r, carry):
        value = front[rows_of(r), :] - dot(lprow[rows_of(r), :], lpcol[...])
        update[rows_of(r), :] = jnp.where(top & (r == 0), 0.0, value)
        return carry

    lax.fori_loop(0, rb, parent_row, 0)

    @pl.when(first)
    def _():
        update[:, 0:BLOCK] = lprow[...]

    @pl.when(corner)
    def _():
        update[0:BLOCK, 0:BLOCK] = kp[...]

    wait_pieces(last)

    for cond, copy in pending:
        pl.when(cond)(copy.wait_send)

    def subtract(r, carry):
        for s in range(1, leaves):
            other[s - 1, rows_of(r), :] = other[s - 1, rows_of(r), :] - corr[s - 1, rows_of(r), :]
        return carry

    lax.fori_loop(0, rb, subtract, 0)


def assemble_kernel(children, sources, where_am_i, update, *refs):
    blocks, out = refs[:children], refs[children]
    r = pl.program_id(0)
    for c in range(out.shape[1] // BLOCK):
        span = slice(c * BLOCK, (c + 1) * BLOCK)
        tile = update[:, span]
        panel = (where_am_i[0] + r == 0) | ((where_am_i[1] == 0) & (c == 0))
        for s in range(children):
            source = sources[s, 1, c]
            keep = (sources[s, 0, r] >= 0) & (source >= 0) & jnp.logical_not(panel)
            at = pl.ds(pl.multiple_of(jnp.maximum(source, 0) * BLOCK, BLOCK), BLOCK)
            tile = tile + jnp.where(keep, blocks[s][:, at], 0.0)
        out[:, span] = tile


def assemble(sources, where_am_i, update, blocks):
    height, breadth = update.shape
    children = len(blocks)

    def moved(s):
        return lambda r, sources, where_am_i: (jnp.maximum(sources[s, 0, r], 0), 0)

    row = pl.BlockSpec((BLOCK, breadth), lambda r, sources, where_am_i: (r, 0))
    return pl.pallas_call(
        functools.partial(assemble_kernel, children),
        grid_spec=pltpu.PrefetchScalarGridSpec(
            num_scalar_prefetch=2,
            grid=(height // BLOCK,),
            in_specs=[row] + [pl.BlockSpec((BLOCK, breadth), moved(s)) for s in range(children)],
            out_specs=row,
        ),
        out_shape=jax.ShapeDtypeStruct((height, breadth), jnp.float32),
        name="assemble",
    )(sources, where_am_i, update, *blocks)


def per_device(sizes, child_fronts, parent_front, block_maps):
    leaves, frows, fcols = sizes
    height, breadth = parent_front.shape
    assert fcols % leaves == 0
    rb, cb = height // BLOCK, breadth // BLOCK
    i, j = lax.axis_index("frow"), lax.axis_index("fcol")
    number = jnp.arange(block_maps.shape[1], dtype=jnp.int32)
    matches = block_maps[0][:, None] == number[None, :]
    inverse = jnp.sum(jnp.where(matches, number[:, None], 0), axis=0)
    deep = -(-max(rb, cb) // 8) * 8
    own_lines, sent_lines = [], []
    for count, position in ((rb, i), (cb, j)):
        source = lax.dynamic_slice_in_dim(inverse, position * count, count)
        kept = source >= CHILD_PANELS
        source = source - position * count
        to = jnp.maximum(inverse[0], CHILD_PANELS)
        swapped = jnp.where(source == to, CHILD_PANELS, jnp.where(source == CHILD_PANELS, to, source))
        swap = (position == 0) & (min(rb, cb) > CHILD_PANELS)
        swapped = jnp.where(swap, swapped, source)
        for lines, values in ((own_lines, source), (sent_lines, swapped)):
            lines.append(jnp.pad(jnp.where(kept, values, -1), (0, deep - count)))
    table, table_send = (
        jnp.broadcast_to(jnp.stack(lines)[:, :, None], (2, deep, BLOCK)) for lines in (own_lines, sent_lines)
    )
    f32 = jnp.float32
    block = jax.ShapeDtypeStruct((height, breadth), f32)
    vmem = pl.BlockSpec(memory_space=pltpu.VMEM)
    sends = (
        leaves * (frows - 1) + 2 * fcols + leaves * CHUNKS * 2 + leaves * fcols + leaves * 7
        + frows + fcols * 3 + 4 + fcols * leaves
    )
    square = (BLOCK, BLOCK)
    scratch = [
        pltpu.VMEM((height, breadth), f32),
        pltpu.VMEM((leaves, WIDE, WIDE), f32),
        pltpu.VMEM((WIDE, WIDE), f32),
        pltpu.VMEM((leaves, height, WIDE), f32),
        pltpu.VMEM((leaves, WIDE, breadth), f32),
        pltpu.VMEM((leaves, height, WIDE), f32),
        pltpu.VMEM((leaves, WIDE, breadth), f32),
        pltpu.VMEM((leaves - 1, height, breadth), f32),
        pltpu.VMEM((WIDE, WIDE), f32),
        pltpu.VMEM((leaves, WIDE, WIDE), f32),
        pltpu.VMEM((height, BLOCK), f32),
        pltpu.VMEM((BLOCK, breadth), f32),
        pltpu.VMEM(square, f32),
        pltpu.VMEM((leaves, height, BLOCK), f32),
        pltpu.VMEM((leaves, BLOCK, breadth), f32),
        pltpu.VMEM(square, f32),
        pltpu.VMEM((height, BLOCK), f32),
        pltpu.VMEM((BLOCK, breadth), f32),
        pltpu.SemaphoreType.DMA((sends,)),
        pltpu.SemaphoreType.DMA((leaves * 14 + 10,)),
    ]
    child, other, update, tables = pl.pallas_call(
        functools.partial(kernel, sizes),
        out_shape=(
            block,
            jax.ShapeDtypeStruct((leaves - 1, height, breadth), f32),
            block,
            jax.ShapeDtypeStruct((leaves - 1, 2, deep, BLOCK), jnp.int32),
        ),
        in_specs=[vmem] * 4,
        out_specs=(vmem,) * 4,
        scratch_shapes=scratch,
        compiler_params=pltpu.CompilerParams(
            collective_id=0, has_side_effects=True, vmem_limit_bytes=56 * 2**20
        ),
        name="fronts",
    )(table, table_send, child_fronts[0], parent_front)
    sources = jnp.concatenate([table[None], tables], axis=0)[:, :, :, 0]
    where_am_i = jnp.stack([i, j]).astype(jnp.int32)
    parent = assemble(sources, where_am_i, update, [child] + [other[s] for s in range(leaves - 1)])
    return child[None], parent


def solution(mesh):
    sizes = (mesh.shape["leaf"], mesh.shape["frow"], mesh.shape["fcol"])
    return jax.shard_map(
        functools.partial(per_device, sizes),
        mesh=mesh,
        in_specs=(P("leaf", "frow", "fcol"), P("frow", "fcol"), P("leaf", None)),
        out_specs=(P("leaf", "frow", "fcol"), P("frow", "fcol")),
        check_vma=False,
    )
```

```python
import functools

import jax
import jax.numpy as jnp
from jax import lax
from jax.experimental import pallas as pl
from jax.experimental.pallas import tpu as pltpu
from jax.sharding import PartitionSpec as P

BLOCK = 128
CHILD_PANELS = 2
WIDE = BLOCK * CHILD_PANELS
CHUNKS = 4
MESH = pl.DeviceIdType.MESH


def dot(a, b, contract=((1,), (0,))):
    return lax.dot_general(
        a, b, (contract, ((), ())),
        precision=lax.Precision.HIGHEST, preferred_element_type=jnp.float32,
    )


def dot_t(a, b):
    return dot(a, b, ((1,), (1,)))


def split(x):
    high = x.astype(jnp.bfloat16)
    return high, (x - high.astype(jnp.float32)).astype(jnp.bfloat16)


def dot_split(a, high, low):
    a_high, a_low = split(a)

    def one(x, y):
        return lax.dot_general(x, y, (((1,), (0,)), ((), ())), preferred_element_type=jnp.float32)

    return one(a_high, high) + (one(a_high, low) + one(a_low, high))


def factor_block(block, between):
    shape = (BLOCK, BLOCK)
    row = lax.broadcasted_iota(jnp.int32, shape, 0)
    lane = lax.broadcasted_iota(jnp.int32, shape, 1)

    def turn(g, carry):
        m, v = carry
        active = row < BLOCK - 8 * g
        for t in range(8):
            scale = 1.0 / m[t : t + 1, t : t + 1]
            column = jnp.where(active & (row > t), jnp.broadcast_to(m[:, t : t + 1], shape), 0.0)
            pivot_m = m[t : t + 1, :] * scale
            pivot_v = v[t : t + 1, :] * scale
            m = m - column * pivot_m
            v = v - column * pivot_v
        m = pltpu.roll(m, BLOCK - 8, 1)
        m = jnp.concatenate([m[8:], m[:8]], axis=0)
        v = jnp.concatenate([v[8:], v[:8]], axis=0)
        return m, v

    carry = (block, jnp.where(row == lane, 1.0, 0.0))
    turns = BLOCK // 8 // CHUNKS
    for q in range(CHUNKS):
        carry = lax.fori_loop(q * turns, (q + 1) * turns, turn, carry)
        between()
    m, v = carry
    root = 1.0 / jnp.sqrt(jnp.sum(jnp.where(row == lane, m, 0.0), axis=1, keepdims=True))
    return jnp.where(lane >= row, m * root, 0.0), v * root


def kernel(sizes, table, table_send, own, front_hbm, child_hbm, other, update_hbm, tables,
           stage, dbuf, piv, rows, cols, left, right, corr, kbuf, wbuf,
           prow, pcol, ppiv, down_part, across, kp, lprow, lpcol, front, child, update, high, low, send_sem, recv_sem, local_sem):
    leaves, frows, fcols = sizes
    height, breadth = own.shape
    rb, cb = height // BLOCK, breadth // BLOCK
    has_c = rb > CHILD_PANELS and cb > CHILD_PANELS
    l, i, j = lax.axis_index("leaf"), lax.axis_index("frow"), lax.axis_index("fcol")
    top, first = i == 0, j == 0
    corner = top & first
    pending = []
    names = {}

    def sem(*name):
        return recv_sem.at[names.setdefault(name, len(names))]

    def start(cond, src, dst, signal, where):
        copy = pltpu.make_async_remote_copy(
            src_ref=src, dst_ref=dst, send_sem=send_sem.at[len(pending)], recv_sem=signal,
            device_id=where, device_id_type=MESH,
        )
        pending.append((cond, copy))
        pl.when(cond)(copy.start)

    def arrived(cond, dst, signal, where):
        copy = pltpu.make_async_remote_copy(
            src_ref=dst, dst_ref=dst, send_sem=send_sem.at[0], recv_sem=signal,
            device_id=where, device_id_type=MESH,
        )
        pl.when(cond)(copy.wait_recv)

    always = i >= 0
    up = {"frow": lax.rem(i + 1, frows)}
    down = {"frow": lax.rem(i + frows - 1, frows)}
    root_row = {"fcol": lax.rem(j + 1, fcols)}

    def leaf_at(s):
        return {"leaf": lax.rem(l + s, leaves)}

    def rows_of(k):
        return pl.ds(pl.multiple_of(k * BLOCK, BLOCK), BLOCK)

    def chunk(ref, q, count):
        size = ref.shape[0] // count
        return ref.at[pl.ds(q * size, size)]

    load = pltpu.make_async_copy(front_hbm, front, local_sem.at[0])
    load.start()

    barrier = pltpu.get_barrier_semaphore()
    for d in range(1, leaves):
        pl.semaphore_signal(barrier, inc=1, device_id=leaf_at(d), device_id_type=MESH)
    for d in range(1, frows):
        pl.semaphore_signal(barrier, inc=1, device_id={"frow": lax.rem(i + d, frows)}, device_id_type=MESH)
    for d in range(1, fcols):
        pl.semaphore_signal(barrier, inc=1, device_id={"fcol": lax.rem(j + d, fcols)}, device_id_type=MESH)
    pl.semaphore_wait(barrier, leaves + frows + fcols - 3)

    pivot_own = own.at[pl.ds(0, WIDE), pl.ds(0, WIDE)]

    def pivot_of(s):
        return pivot_own if s == 0 else other.at[s - 1, pl.ds(0, WIDE), pl.ds(0, WIDE)]

    def send_pivot(s):
        for b in range(1, frows):
            start(corner, pivot_of(s), dbuf.at[s], sem("d", s), {"frow": b})
        for c in range(1, fcols):
            if c % leaves == s:
                start(corner, pivot_of(s), piv, sem("piv"), {"fcol": c})

    def pass_pivot(s):
        inner = first & (i > 0)
        arrived(inner, dbuf.at[s], sem("d", s), down)
        for c in range(1, fcols):
            if c % leaves == s:
                start(inner, dbuf.at[s], piv, sem("piv"), {"fcol": c})

    send_pivot(0)
    for q in range(CHUNKS):
        start(top, chunk(own.at[pl.ds(0, WIDE)], q, CHUNKS), chunk(cols.at[0], q, CHUNKS), sem("c", 0, q), up)
    for c in range(1, fcols):
        start(first, own.at[:, pl.ds(0, WIDE)], rows.at[0], sem("r", 0), {"fcol": c})

    def is_at(ref, kind, k, t, shape):
        return jnp.broadcast_to(ref[kind, pl.ds(k, 1), 0:1], shape) == t

    def chosen(ref, kind, k, count, block):
        total = 0.0
        for t in range(count):
            part = block(t)
            total = total + jnp.where(is_at(ref, kind, k, t, part.shape), part, 0.0)
        return total

    def stage_rows(r, carry):
        stage[rows_of(r), :] = own[rows_of(r), :]
        return carry

    def block_slice(t):
        return slice(t * BLOCK, (t + 1) * BLOCK)

    def stage_cols(r, carry):
        held = stage[rows_of(r), block_slice(CHILD_PANELS)]
        value = held
        for t in range(CHILD_PANELS + 1, cb):
            here = stage[rows_of(r), block_slice(t)]
            match = is_at(table, 1, 0, t, here.shape)
            value = jnp.where(match, here, value)
            stage[rows_of(r), block_slice(t)] = jnp.where(match, held, here)
        stage[rows_of(r), block_slice(CHILD_PANELS)] = value
        return carry

    three = WIDE + BLOCK
    pieces = [(0, WIDE, 0, WIDE), (0, WIDE, WIDE, breadth)]
    if height > WIDE:
        pieces += [(WIDE, height, 0, WIDE), (WIDE, three, WIDE, breadth)]
    if height > three:
        pieces += [(three, height, WIDE, three), (three, height, three, breadth)]
    panel, middle, last = [2], [3, 4], [5]
    panel, middle, last = ([n for n in some if n < len(pieces)] for some in (panel, middle, last))

    def piece(ref, n):
        a, b, c, d = pieces[n]
        return ref.at[pl.ds(a, b - a), pl.ds(c, d - c)]

    def send_pieces(numbers, cond=always, source=stage):
        for n in numbers:
            for s in range(1, leaves):
                start(cond, piece(source, n), piece(other.at[s - 1], n), sem("y", s, n), leaf_at(s))

    def wait_pieces(numbers):
        for n in numbers:
            for s in range(1, leaves):
                arrived(always, piece(other.at[s - 1], n), sem("y", s, n), leaf_at(leaves - s))

    for s in range(1, leaves):
        start(always, table_send, tables.at[s - 1], sem("tables", s), leaf_at(s))
    send_pieces([0], source=own)
    send_pieces(panel, i > 0, own)
    lax.fori_loop(0, CHILD_PANELS, stage_rows, 0)
    if has_c:
        @pl.when(first)
        def _():
            lax.fori_loop(0, CHILD_PANELS, stage_cols, 0)
    send_pieces([1], top)
    lax.fori_loop(CHILD_PANELS, rb, stage_rows, 0)
    if has_c:
        @pl.when(top)
        def _():
            def fix(c, carry):
                held = own[block_slice(CHILD_PANELS), rows_of(c)]
                value = held
                for t in range(CHILD_PANELS + 1, rb):
                    here = own[block_slice(t), rows_of(c)]
                    match = is_at(table, 0, 0, t, here.shape)
                    value = jnp.where(match, here, value)
                    stage[block_slice(t), rows_of(c)] = jnp.where(match, held, here)
                stage[block_slice(CHILD_PANELS), rows_of(c)] = value
                return carry

            lax.fori_loop(0, cb, fix, 0)

        @pl.when(first)
        def _():
            lax.fori_loop(CHILD_PANELS, rb, stage_cols, 0)
    send_pieces(panel, top)
    send_pieces(middle[1:], i > 0)
    send_pieces([1], i > 0)
    send_pieces(middle, top)
    send_pieces(middle[:1], i > 0)
    send_pieces(last)

    @pl.when(top)
    def _():
        cols[0] = own[0:WIDE, :]

    @pl.when(first)
    def _():
        rows[0] = own[:, 0:WIDE]

    pass_pivot(0)

    @pl.when(corner)
    def _():
        piv[...] = own[0:WIDE, 0:WIDE]

    @pl.when(first & (i > 0))
    def _():
        piv[...] = dbuf[0]

    inner_rows = (i > 0) & (i < frows - 1)

    def pass_cols(s, q):
        here = chunk(cols.at[s], q, CHUNKS)
        arrived(inner_rows, here, sem("c", s, q), down)
        start(inner_rows, here, here, sem("c", s, q), up)

    wait_pieces([0])
    for s in range(1, leaves):
        send_pivot(s)
    for s in range(1, leaves):
        pass_pivot(s)

    arrived(j > 0, piv, sem("piv"), root_row)
    slot = lax.rem(j, leaves)
    base = j - slot
    step = []

    def between():
        n = len(step)
        step.append(n)
        q = n % CHUNKS
        if n < CHUNKS:
            pass_cols(0, q)
        else:
            for s in range(1, leaves):
                pass_cols(s, q)
        if n == CHUNKS - 1:
            wait_pieces([1])
            for s in range(1, leaves):
                for p in range(CHUNKS):
                    source = chunk(other.at[s - 1, pl.ds(0, WIDE)], p, CHUNKS)
                    start(top, source, chunk(cols.at[s], p, CHUNKS), sem("c", s, p), up)

                @pl.when(top)
                def _(s=s):
                    cols[s] = other[s - 1, 0:WIDE, :]
        if n == CHUNKS + 1:
            wait_pieces(panel)
            for s in range(1, leaves):
                for c in range(1, fcols):
                    start(first, other.at[s - 1, :, pl.ds(0, WIDE)], rows.at[s], sem("r", s), {"fcol": c})

                @pl.when(first)
                def _(s=s):
                    rows[s] = other[s - 1, :, 0:WIDE]

    lo, hi = slice(0, BLOCK), slice(BLOCK, WIDE)
    upper, inverse = factor_block(piv[lo, lo], between)
    kbuf[...] = jnp.zeros_like(kbuf)
    kbuf[lo, lo] = upper.T
    wbuf[slot, lo, lo] = inverse
    wbuf[slot, lo, hi] = jnp.zeros((BLOCK, BLOCK), jnp.float32)
    below = dot_t(piv[hi, lo], inverse)
    kbuf[hi, lo] = below
    upper, second = factor_block(piv[hi, hi] - dot_t(below, below), between)
    kbuf[hi, hi] = upper.T
    wbuf[slot, hi, hi] = second
    wbuf[slot, hi, lo] = -dot(second, dot(below, inverse))
    w_sems = [sem("w", s) for s in range(leaves)]
    w_first = names[("w", 0)]
    for d in range(1, leaves):
        start(always, wbuf.at[slot], wbuf.at[slot], recv_sem.at[w_first + slot], {"fcol": base + lax.rem(slot + d, leaves)})
    for d in range(1, leaves):
        from_slot = lax.rem(slot + d, leaves)
        arrived(always, wbuf.at[from_slot], recv_sem.at[w_first + from_slot], {"fcol": base + from_slot})

    for s in range(1, leaves):
        arrived(always, tables.at[s - 1], sem("tables", s), leaf_at(leaves - s))

    def make_panels(s):
        arrived(j > 0, rows.at[s], sem("r", s), root_row)
        for q in range(CHUNKS):
            arrived(i == frows - 1, chunk(cols.at[s], q, CHUNKS), sem("c", s, q), down)

        def wide(k):
            return pl.ds(pl.multiple_of(k * WIDE, WIDE), WIDE)

        def one_row(r, carry):
            left[s, wide(r), :] = dot_t(rows[s, wide(r), :], wbuf[s])
            return carry

        def one_col(c, carry):
            right[s, :, wide(c)] = dot(wbuf[s], cols[s, :, wide(c)])
            return carry

        lax.fori_loop(0, height // WIDE, one_row, 0)
        lax.fori_loop(0, breadth // WIDE, one_col, 0)

    make_panels(0)
    high[...], low[...] = split(right[0])

    def child_row(r, carry):
        value = own[rows_of(r), :] - dot_split(left[0, rows_of(r), :], high[...], low[...])
        child[rows_of(r), :] = jnp.where(top & (r < CHILD_PANELS), 0.0, value)
        return carry

    lax.fori_loop(0, rb, child_row, 0)

    @pl.when(first)
    def _():
        child[:, 0:WIDE] = left[0]

    @pl.when(corner)
    def _():
        child[0:WIDE, 0:WIDE] = kbuf[...]

    child_copy = pltpu.make_async_copy(child, child_hbm, local_sem.at[1])
    child_copy.start()
    for s in range(1, leaves):
        make_panels(s)
    wait_pieces(middle)
    load.wait()

    third = block_slice(CHILD_PANELS)
    known = [table] + [tables.at[s - 1] for s in range(1, leaves)]

    @pl.when(first)
    def _():
        for s in range(leaves if has_c else 0):
            if s == 0:
                beside = chosen(table, 1, 0, cb, lambda t: right[0, :, block_slice(t)])
            else:
                beside = right[s, :, third]
                beside = jnp.where(is_at(known[s], 1, 0, CHILD_PANELS, beside.shape), beside, 0.0)

            def one(r, carry, s=s, beside=beside):
                if s == 0:
                    raw = chosen(table, 1, 0, cb, lambda t: own[rows_of(r), block_slice(t)])
                else:
                    raw = other[s - 1, rows_of(r), third]
                    raw = jnp.where(is_at(known[s], 1, 0, CHILD_PANELS, raw.shape), raw, 0.0)
                down_part[s, rows_of(r), :] = raw - dot(left[s, rows_of(r), :], beside)
                return carry

            lax.fori_loop(0, rb, one, 0)

        def assemble(r, carry):
            tile = front[rows_of(r), 0:BLOCK]
            for s in range(leaves if has_c else 0):
                tile = tile + chosen(known[s], 0, r, rb, lambda t: down_part[s, block_slice(t), :])
            prow[rows_of(r), :] = tile
            return carry

        lax.fori_loop(0, rb, assemble, 0)

    @pl.when(top)
    def _():
        for s in range(leaves if has_c else 0):
            if s == 0:
                beside = chosen(table, 0, 0, rb, lambda t: left[0, block_slice(t), :])
            else:
                beside = left[s, third, :]
                beside = jnp.where(is_at(known[s], 0, 0, CHILD_PANELS, beside.shape), beside, 0.0)

            def one(c, carry, s=s, beside=beside):
                if s == 0:
                    raw = chosen(table, 0, 0, rb, lambda t: own[block_slice(t), rows_of(c)])
                else:
                    raw = other[s - 1, third, rows_of(c)]
                    raw = jnp.where(is_at(known[s], 0, 0, CHILD_PANELS, raw.shape), raw, 0.0)
                across[s, :, rows_of(c)] = raw - dot(beside, right[s, :, rows_of(c)])
                return carry

            lax.fori_loop(0, cb, one, 0)

        def assemble(c, carry):
            tile = front[0:BLOCK, rows_of(c)]
            for s in range(leaves if has_c else 0):
                tile = tile + chosen(known[s], 1, c, cb, lambda t: across[s, :, block_slice(t)])
            pcol[:, rows_of(c)] = tile
            return carry

        lax.fori_loop(0, cb, assemble, 0)

    @pl.when(corner)
    def _():
        ppiv[...] = prow[0:BLOCK, :]

    for b in range(1, frows):
        start(corner, ppiv, ppiv, sem("pp"), {"frow": b})
    for c in range(1, fcols):
        start(corner, ppiv, ppiv, sem("pp"), {"fcol": c})
    for q in range(2):
        start(top, chunk(pcol, q, 2), chunk(pcol, q, 2), sem("pc", q), up)
    for c in range(1, fcols):
        start(first, prow, prow, sem("pr"), {"fcol": c})
    arrived(first & (i > 0), ppiv, sem("pp"), down)
    for c in range(1, fcols):
        start(first & (i > 0), ppiv, ppiv, sem("pp"), {"fcol": c})

    for s in range(1, leaves):
        high[...], low[...] = split(right[s])

        def corr_row(r, carry, s=s):
            corr[s - 1, rows_of(r), :] = dot_split(left[s, rows_of(r), :], high[...], low[...])
            return carry

        lax.fori_loop(0, rb, corr_row, 0)

    arrived(j > 0, ppiv, sem("pp"), root_row)
    turn = []

    def pass_parent():
        n = len(turn)
        turn.append(n)
        if n % 2 == 0:
            part = chunk(pcol, n // 2, 2)
            arrived(inner_rows, part, sem("pc", n // 2), down)
            start(inner_rows, part, part, sem("pc", n // 2), up)

    upper, inverse = factor_block(ppiv[...], pass_parent)
    kp[...] = upper.T
    for q in range(2):
        arrived(i == frows - 1, chunk(pcol, q, 2), sem("pc", q), down)
    arrived(j > 0, prow, sem("pr"), root_row)
    lprow[...] = dot_t(prow[...], inverse)
    lpcol[...] = dot(inverse, pcol[...])
    high[0:BLOCK, :], low[0:BLOCK, :] = split(lpcol[...])

    def parent_row(r, carry):
        value = front[rows_of(r), :] - dot_split(lprow[rows_of(r), :], high[0:BLOCK, :], low[0:BLOCK, :])
        update[rows_of(r), :] = jnp.where(top & (r == 0), 0.0, value)
        return carry

    lax.fori_loop(0, rb, parent_row, 0)

    @pl.when(first)
    def _():
        update[:, 0:BLOCK] = lprow[...]

    @pl.when(corner)
    def _():
        update[0:BLOCK, 0:BLOCK] = kp[...]

    update_copy = pltpu.make_async_copy(update, update_hbm, local_sem.at[2])
    update_copy.start()
    wait_pieces(last)

    for cond, copy in pending:
        pl.when(cond)(copy.wait_send)

    def subtract(r, carry):
        for s in range(1, leaves):
            other[s - 1, rows_of(r), :] = other[s - 1, rows_of(r), :] - corr[s - 1, rows_of(r), :]
        return carry

    lax.fori_loop(0, rb, subtract, 0)
    child_copy.wait()
    update_copy.wait()


def assemble_kernel(children, sources, where_am_i, update, *refs):
    blocks, same, out, child = refs[:children], *refs[children:]
    child[...] = same[...]
    r = pl.program_id(0)
    for c in range(out.shape[1] // BLOCK):
        span = slice(c * BLOCK, (c + 1) * BLOCK)
        tile = update[:, span]
        panel = (where_am_i[0] + r == 0) | ((where_am_i[1] == 0) & (c == 0))
        for s in range(children):
            source = sources[s, 1, c]
            keep = (sources[s, 0, r] >= 0) & (source >= 0) & jnp.logical_not(panel)
            at = pl.ds(pl.multiple_of(jnp.maximum(source, 0) * BLOCK, BLOCK), BLOCK)
            tile = tile + jnp.where(keep, blocks[s][:, at], 0.0)
        out[:, span] = tile


def assemble(sources, where_am_i, update, blocks):
    height, breadth = update.shape
    children = len(blocks)

    def moved(s):
        return lambda r, sources, where_am_i: (jnp.maximum(sources[s, 0, r], 0), 0)

    row = pl.BlockSpec((BLOCK, breadth), lambda r, sources, where_am_i: (r, 0))
    return pl.pallas_call(
        functools.partial(assemble_kernel, children),
        grid_spec=pltpu.PrefetchScalarGridSpec(
            num_scalar_prefetch=2,
            grid=(height // BLOCK,),
            in_specs=[row] + [pl.BlockSpec((BLOCK, breadth), moved(s)) for s in range(children)] + [row],
            out_specs=(row, row),
        ),
        out_shape=(jax.ShapeDtypeStruct((height, breadth), jnp.float32),) * 2,
        name="assemble",
    )(sources, where_am_i, update, *blocks, blocks[0])


def per_device(sizes, child_fronts, parent_front, block_maps):
    leaves, frows, fcols = sizes
    height, breadth = parent_front.shape
    assert fcols % leaves == 0
    rb, cb = height // BLOCK, breadth // BLOCK
    i, j = lax.axis_index("frow"), lax.axis_index("fcol")
    number = jnp.arange(block_maps.shape[1], dtype=jnp.int32)
    matches = block_maps[0][:, None] == number[None, :]
    inverse = jnp.sum(jnp.where(matches, number[:, None], 0), axis=0)
    deep = -(-max(rb, cb) // 8) * 8
    own_lines, sent_lines = [], []
    for count, position in ((rb, i), (cb, j)):
        source = lax.dynamic_slice_in_dim(inverse, position * count, count)
        kept = source >= CHILD_PANELS
        source = source - position * count
        to = jnp.maximum(inverse[0], CHILD_PANELS)
        swapped = jnp.where(source == to, CHILD_PANELS, jnp.where(source == CHILD_PANELS, to, source))
        swap = (position == 0) & (min(rb, cb) > CHILD_PANELS)
        swapped = jnp.where(swap, swapped, source)
        for lines, values in ((own_lines, source), (sent_lines, swapped)):
            lines.append(jnp.pad(jnp.where(kept, values, -1), (0, deep - count)))
    table, table_send = (
        jnp.broadcast_to(jnp.stack(lines)[:, :, None], (2, deep, BLOCK)) for lines in (own_lines, sent_lines)
    )
    f32 = jnp.float32
    block = jax.ShapeDtypeStruct((height, breadth), f32)
    vmem, away = pl.BlockSpec(memory_space=pltpu.VMEM), pl.BlockSpec(memory_space=pl.ANY)
    sends = (
        leaves * (frows - 1) + 2 * fcols + leaves * CHUNKS * 2 + leaves * fcols + leaves * 7
        + frows + fcols * 3 + 4 + fcols * leaves
    )
    square = (BLOCK, BLOCK)
    scratch = [
        pltpu.VMEM((height, breadth), f32),
        pltpu.VMEM((leaves, WIDE, WIDE), f32),
        pltpu.VMEM((WIDE, WIDE), f32),
        pltpu.VMEM((leaves, height, WIDE), f32),
        pltpu.VMEM((leaves, WIDE, breadth), f32),
        pltpu.VMEM((leaves, height, WIDE), f32),
        pltpu.VMEM((leaves, WIDE, breadth), f32),
        pltpu.VMEM((leaves - 1, height, breadth), f32),
        pltpu.VMEM((WIDE, WIDE), f32),
        pltpu.VMEM((leaves, WIDE, WIDE), f32),
        pltpu.VMEM((height, BLOCK), f32),
        pltpu.VMEM((BLOCK, breadth), f32),
        pltpu.VMEM(square, f32),
        pltpu.VMEM((leaves, height, BLOCK), f32),
        pltpu.VMEM((leaves, BLOCK, breadth), f32),
        pltpu.VMEM(square, f32),
        pltpu.VMEM((height, BLOCK), f32),
        pltpu.VMEM((BLOCK, breadth), f32),
        pltpu.VMEM((height, breadth), f32),
        pltpu.VMEM((height, breadth), f32),
        pltpu.VMEM((height, breadth), f32),
        pltpu.VMEM((WIDE, breadth), jnp.bfloat16),
        pltpu.VMEM((WIDE, breadth), jnp.bfloat16),
        pltpu.SemaphoreType.DMA((sends,)),
        pltpu.SemaphoreType.DMA((leaves * 14 + 10,)),
        pltpu.SemaphoreType.DMA((3,)),
    ]
    child, other, update, tables = pl.pallas_call(
        functools.partial(kernel, sizes),
        out_shape=(
            block,
            jax.ShapeDtypeStruct((leaves - 1, height, breadth), f32),
            block,
            jax.ShapeDtypeStruct((leaves - 1, 2, deep, BLOCK), jnp.int32),
        ),
        in_specs=[vmem] * 3 + [away],
        out_specs=(away, vmem, away, vmem),
        scratch_shapes=scratch,
        compiler_params=pltpu.CompilerParams(
            collective_id=0, has_side_effects=True, vmem_limit_bytes=56 * 2**20
        ),
        name="fronts",
    )(table, table_send, child_fronts[0], parent_front)
    sources = jnp.concatenate([table[None], tables], axis=0)[:, :, :, 0]
    where_am_i = jnp.stack([i, j]).astype(jnp.int32)
    parent, child = assemble(sources, where_am_i, update, [child] + [other[s] for s in range(leaves - 1)])
    return child[None], parent


def solution(mesh):
    sizes = (mesh.shape["leaf"], mesh.shape["frow"], mesh.shape["fcol"])
    return jax.shard_map(
        functools.partial(per_device, sizes),
        mesh=mesh,
        in_specs=(P("leaf", "frow", "fcol"), P("frow", "fcol"), P("leaf", None)),
        out_specs=(P("leaf", "frow", "fcol"), P("frow", "fcol")),
        check_vma=False,
    )
```

```python
import functools

import jax
import jax.numpy as jnp
from jax import lax
from jax.experimental import pallas as pl
from jax.experimental.pallas import tpu as pltpu
from jax.sharding import PartitionSpec as P

BLOCK = 128
CHILD_PANELS = 2
WIDE = BLOCK * CHILD_PANELS
CHUNKS = 4
MESH = pl.DeviceIdType.MESH


def dot(a, b, contract=((1,), (0,))):
    return lax.dot_general(
        a, b, (contract, ((), ())),
        precision=lax.Precision.HIGHEST, preferred_element_type=jnp.float32,
    )


def dot_t(a, b):
    return dot(a, b, ((1,), (1,)))


def split(x):
    high = x.astype(jnp.bfloat16)
    return high, (x - high.astype(jnp.float32)).astype(jnp.bfloat16)


def dot_split(a, high, low):
    a_high, a_low = split(a)

    def one(x, y):
        return lax.dot_general(x, y, (((1,), (0,)), ((), ())), preferred_element_type=jnp.float32)

    return one(a_high, high) + (one(a_high, low) + one(a_low, high))


def factor_block(block, between):
    shape = (BLOCK, BLOCK)
    row = lax.broadcasted_iota(jnp.int32, shape, 0)
    lane = lax.broadcasted_iota(jnp.int32, shape, 1)

    def turn(g, carry):
        m, v = carry
        active = row < BLOCK - 8 * g
        for t in range(8):
            scale = 1.0 / m[t : t + 1, t : t + 1]
            column = jnp.where(active & (row > t), jnp.broadcast_to(m[:, t : t + 1], shape), 0.0)
            pivot_m = m[t : t + 1, :] * scale
            pivot_v = v[t : t + 1, :] * scale
            m = m - column * pivot_m
            v = v - column * pivot_v
        m = pltpu.roll(m, BLOCK - 8, 1)
        m = jnp.concatenate([m[8:], m[:8]], axis=0)
        v = jnp.concatenate([v[8:], v[:8]], axis=0)
        return m, v

    carry = (block, jnp.where(row == lane, 1.0, 0.0))
    turns = BLOCK // 8 // CHUNKS
    for q in range(CHUNKS):
        carry = lax.fori_loop(q * turns, (q + 1) * turns, turn, carry)
        between()
    m, v = carry
    root = 1.0 / jnp.sqrt(jnp.sum(jnp.where(row == lane, m, 0.0), axis=1, keepdims=True))
    return jnp.where(lane >= row, m * root, 0.0), v * root


def kernel(sizes, table, table_send, own, front_hbm, child_hbm, other, update_hbm, tables,
           stage, dbuf, piv, rows, cols, left, right, corr, kbuf, wbuf,
           prow, pcol, ppiv, down_part, across, kp, lprow, lpcol, front, child, update, high, low, send_sem, recv_sem, local_sem):
    leaves, frows, fcols = sizes
    height, breadth = own.shape
    rb, cb = height // BLOCK, breadth // BLOCK
    has_c = rb > CHILD_PANELS and cb > CHILD_PANELS
    l, i, j = lax.axis_index("leaf"), lax.axis_index("frow"), lax.axis_index("fcol")
    top, first = i == 0, j == 0
    corner = top & first
    pending = []
    names = {}

    def sem(*name):
        return recv_sem.at[names.setdefault(name, len(names))]

    def start(cond, src, dst, signal, where):
        copy = pltpu.make_async_remote_copy(
            src_ref=src, dst_ref=dst, send_sem=send_sem.at[len(pending)], recv_sem=signal,
            device_id=where, device_id_type=MESH,
        )
        pending.append((cond, copy))
        pl.when(cond)(copy.start)

    def arrived(cond, dst, signal, where):
        copy = pltpu.make_async_remote_copy(
            src_ref=dst, dst_ref=dst, send_sem=send_sem.at[0], recv_sem=signal,
            device_id=where, device_id_type=MESH,
        )
        pl.when(cond)(copy.wait_recv)

    always = i >= 0
    up = {"frow": lax.rem(i + 1, frows)}
    down = {"frow": lax.rem(i + frows - 1, frows)}
    root_row = {"fcol": lax.rem(j + 1, fcols)}

    def leaf_at(s):
        return {"leaf": lax.rem(l + s, leaves)}

    def rows_of(k):
        return pl.ds(pl.multiple_of(k * BLOCK, BLOCK), BLOCK)

    def chunk(ref, q, count):
        size = ref.shape[0] // count
        return ref.at[pl.ds(q * size, size)]

    load = pltpu.make_async_copy(front_hbm, front, local_sem.at[0])
    load.start()

    barrier = pltpu.get_barrier_semaphore()
    for d in range(1, leaves):
        pl.semaphore_signal(barrier, inc=1, device_id=leaf_at(d), device_id_type=MESH)
    for d in range(1, frows):
        pl.semaphore_signal(barrier, inc=1, device_id={"frow": lax.rem(i + d, frows)}, device_id_type=MESH)
    for d in range(1, fcols):
        pl.semaphore_signal(barrier, inc=1, device_id={"fcol": lax.rem(j + d, fcols)}, device_id_type=MESH)
    pl.semaphore_wait(barrier, leaves + frows + fcols - 3)

    pivot_own = own.at[pl.ds(0, WIDE), pl.ds(0, WIDE)]

    def pivot_of(s):
        return pivot_own if s == 0 else other.at[s - 1, pl.ds(0, WIDE), pl.ds(0, WIDE)]

    def send_pivot(s):
        for b in range(1, frows):
            start(corner, pivot_of(s), dbuf.at[s], sem("d", s), {"frow": b})
        for c in range(1, fcols):
            if c % leaves == s:
                start(corner, pivot_of(s), piv, sem("piv"), {"fcol": c})

    def pass_pivot(s):
        inner = first & (i > 0)
        arrived(inner, dbuf.at[s], sem("d", s), down)
        for c in range(1, fcols):
            if c % leaves == s:
                start(inner, dbuf.at[s], piv, sem("piv"), {"fcol": c})

    send_pivot(0)
    for q in range(CHUNKS):
        start(top, chunk(own.at[pl.ds(0, WIDE)], q, CHUNKS), chunk(cols.at[0], q, CHUNKS), sem("c", 0, q), up)
    half = height // 2

    def send_rows(s, source):
        for c in range(1, fcols):
            if c == 1:
                start(first, source, rows.at[s], sem("r", s), {"fcol": c})
            else:
                part = pl.ds(c % 2 * half, half)
                start(first, source.at[part], rows.at[s, part], sem("r", s), {"fcol": c})

    def take_rows(s):
        partner = {"fcol": j + 1 - 2 * lax.rem(j, 2)}
        mine = rows.at[s, pl.ds(pl.multiple_of(lax.rem(j, 2) * half, 8), half)]
        theirs = rows.at[s, pl.ds(pl.multiple_of((1 - lax.rem(j, 2)) * half, 8), half)]
        arrived(j == 1, rows.at[s], sem("r", s), root_row)
        arrived(j > 1, mine, sem("r", s), root_row)
        start(j > 1, mine, mine, sem("r2", s), partner)
        arrived(j > 1, theirs, sem("r2", s), partner)

    send_rows(0, own.at[:, pl.ds(0, WIDE)])

    def is_at(ref, kind, k, t, shape):
        return jnp.broadcast_to(ref[kind, pl.ds(k, 1), 0:1], shape) == t

    def chosen(ref, kind, k, count, block):
        total = 0.0
        for t in range(count):
            part = block(t)
            total = total + jnp.where(is_at(ref, kind, k, t, part.shape), part, 0.0)
        return total

    def stage_rows(r, carry):
        stage[rows_of(r), :] = own[rows_of(r), :]
        return carry

    def block_slice(t):
        return slice(t * BLOCK, (t + 1) * BLOCK)

    def stage_cols(r, carry):
        held = stage[rows_of(r), block_slice(CHILD_PANELS)]
        value = held
        for t in range(CHILD_PANELS + 1, cb):
            here = stage[rows_of(r), block_slice(t)]
            match = is_at(table, 1, 0, t, here.shape)
            value = jnp.where(match, here, value)
            stage[rows_of(r), block_slice(t)] = jnp.where(match, held, here)
        stage[rows_of(r), block_slice(CHILD_PANELS)] = value
        return carry

    three = WIDE + BLOCK
    pieces = [(0, WIDE, 0, WIDE), (0, WIDE, WIDE, breadth)]
    if height > WIDE:
        pieces += [(WIDE, height, 0, WIDE), (WIDE, three, WIDE, breadth)]
    if height > three:
        pieces += [(three, height, WIDE, three), (three, height, three, breadth)]
    panel, middle, last = [2], [3, 4], [5]
    panel, middle, last = ([n for n in some if n < len(pieces)] for some in (panel, middle, last))

    def piece(ref, n):
        a, b, c, d = pieces[n]
        return ref.at[pl.ds(a, b - a), pl.ds(c, d - c)]

    def send_pieces(numbers, cond=always, source=stage):
        for n in numbers:
            for s in range(1, leaves):
                start(cond, piece(source, n), piece(other.at[s - 1], n), sem("y", s, n), leaf_at(s))

    def wait_pieces(numbers, cond=always):
        for n in numbers:
            for s in range(1, leaves):
                arrived(cond, piece(other.at[s - 1], n), sem("y", s, n), leaf_at(leaves - s))

    for s in range(1, leaves):
        start(always, table_send, tables.at[s - 1], sem("tables", s), leaf_at(s))
    send_pieces([0], source=own)
    send_pieces(panel, i > 0, own)
    lax.fori_loop(0, CHILD_PANELS, stage_rows, 0)
    if has_c:
        @pl.when(first)
        def _():
            lax.fori_loop(0, CHILD_PANELS, stage_cols, 0)
    send_pieces([1], top)
    lax.fori_loop(CHILD_PANELS, rb, stage_rows, 0)
    if has_c:
        @pl.when(top)
        def _():
            def fix(c, carry):
                held = own[block_slice(CHILD_PANELS), rows_of(c)]
                value = held
                for t in range(CHILD_PANELS + 1, rb):
                    here = own[block_slice(t), rows_of(c)]
                    match = is_at(table, 0, 0, t, here.shape)
                    value = jnp.where(match, here, value)
                    stage[block_slice(t), rows_of(c)] = jnp.where(match, held, here)
                stage[block_slice(CHILD_PANELS), rows_of(c)] = value
                return carry

            lax.fori_loop(0, cb, fix, 0)

        @pl.when(first)
        def _():
            lax.fori_loop(CHILD_PANELS, rb, stage_cols, 0)
    send_pieces(panel, top)
    send_pieces(middle[1:], i > 0)
    send_pieces([1], i > 0)
    send_pieces(middle, top)
    send_pieces(middle[:1], i > 0)
    send_pieces(last)

    @pl.when(top)
    def _():
        cols[0] = own[0:WIDE, :]

    @pl.when(first)
    def _():
        rows[0] = own[:, 0:WIDE]

    pass_pivot(0)

    @pl.when(corner)
    def _():
        piv[...] = own[0:WIDE, 0:WIDE]

    @pl.when(first & (i > 0))
    def _():
        piv[...] = dbuf[0]

    inner_rows = (i > 0) & (i < frows - 1)

    def pass_cols(s, q):
        here = chunk(cols.at[s], q, CHUNKS)
        arrived(inner_rows, here, sem("c", s, q), down)
        start(inner_rows, here, here, sem("c", s, q), up)

    edge = top | first
    inside = (i > 0) & (j > 0)
    wait_pieces([0], edge)
    for s in range(1, leaves):
        send_pivot(s)
    for s in range(1, leaves):
        pass_pivot(s)

    arrived(j > 0, piv, sem("piv"), root_row)
    slot = lax.rem(j, leaves)
    base = j - slot
    step = []

    def between():
        n = len(step)
        step.append(n)
        q = n % CHUNKS
        if n < CHUNKS:
            pass_cols(0, q)
        else:
            for s in range(1, leaves):
                pass_cols(s, q)
        if n == CHUNKS - 1:
            wait_pieces([1], top)
            for s in range(1, leaves):
                for p in range(CHUNKS):
                    source = chunk(other.at[s - 1, pl.ds(0, WIDE)], p, CHUNKS)
                    start(top, source, chunk(cols.at[s], p, CHUNKS), sem("c", s, p), up)

                @pl.when(top)
                def _(s=s):
                    cols[s] = other[s - 1, 0:WIDE, :]
        if n == CHUNKS + 1:
            wait_pieces(panel, first)
            for s in range(1, leaves):
                send_rows(s, other.at[s - 1, :, pl.ds(0, WIDE)])

                @pl.when(first)
                def _(s=s):
                    rows[s] = other[s - 1, :, 0:WIDE]

    lo, hi = slice(0, BLOCK), slice(BLOCK, WIDE)
    upper, inverse = factor_block(piv[lo, lo], between)
    kbuf[...] = jnp.zeros_like(kbuf)
    kbuf[lo, lo] = upper.T
    wbuf[slot, lo, lo] = inverse
    wbuf[slot, lo, hi] = jnp.zeros((BLOCK, BLOCK), jnp.float32)
    below = dot_t(piv[hi, lo], inverse)
    kbuf[hi, lo] = below
    upper, second = factor_block(piv[hi, hi] - dot_t(below, below), between)
    kbuf[hi, hi] = upper.T
    wbuf[slot, hi, hi] = second
    wbuf[slot, hi, lo] = -dot(second, dot(below, inverse))
    w_sems = [sem("w", s) for s in range(leaves)]
    w_first = names[("w", 0)]
    for d in range(1, leaves):
        start(always, wbuf.at[slot], wbuf.at[slot], recv_sem.at[w_first + slot], {"fcol": base + lax.rem(slot + d, leaves)})
    for d in range(1, leaves):
        from_slot = lax.rem(slot + d, leaves)
        arrived(always, wbuf.at[from_slot], recv_sem.at[w_first + from_slot], {"fcol": base + from_slot})

    for s in range(1, leaves):
        arrived(always, tables.at[s - 1], sem("tables", s), leaf_at(leaves - s))

    def make_panels(s):
        take_rows(s)
        for q in range(CHUNKS):
            arrived(i == frows - 1, chunk(cols.at[s], q, CHUNKS), sem("c", s, q), down)

        def wide(k):
            return pl.ds(pl.multiple_of(k * WIDE, WIDE), WIDE)

        def one_row(r, carry):
            left[s, wide(r), :] = dot_t(rows[s, wide(r), :], wbuf[s])
            return carry

        def one_col(c, carry):
            right[s, :, wide(c)] = dot(wbuf[s], cols[s, :, wide(c)])
            return carry

        lax.fori_loop(0, height // WIDE, one_row, 0)
        lax.fori_loop(0, breadth // WIDE, one_col, 0)

    make_panels(0)
    high[...], low[...] = split(right[0])

    def child_row(r, carry):
        value = own[rows_of(r), :] - dot_split(left[0, rows_of(r), :], high[...], low[...])
        child[rows_of(r), :] = jnp.where(top & (r < CHILD_PANELS), 0.0, value)
        return carry

    lax.fori_loop(0, rb, child_row, 0)

    @pl.when(first)
    def _():
        child[:, 0:WIDE] = left[0]

    @pl.when(corner)
    def _():
        child[0:WIDE, 0:WIDE] = kbuf[...]

    child_copy = pltpu.make_async_copy(child, child_hbm, local_sem.at[1])
    child_copy.start()
    for s in range(1, leaves):
        make_panels(s)
    wait_pieces([1], first & (i > 0))
    wait_pieces(panel, top & (j > 0))
    wait_pieces(middle, edge)
    load.wait()

    third = block_slice(CHILD_PANELS)
    known = [table] + [tables.at[s - 1] for s in range(1, leaves)]

    @pl.when(first)
    def _():
        for s in range(leaves if has_c else 0):
            if s == 0:
                beside = chosen(table, 1, 0, cb, lambda t: right[0, :, block_slice(t)])
            else:
                beside = right[s, :, third]
                beside = jnp.where(is_at(known[s], 1, 0, CHILD_PANELS, beside.shape), beside, 0.0)

            def one(r, carry, s=s, beside=beside):
                if s == 0:
                    raw = chosen(table, 1, 0, cb, lambda t: own[rows_of(r), block_slice(t)])
                else:
                    raw = other[s - 1, rows_of(r), third]
                    raw = jnp.where(is_at(known[s], 1, 0, CHILD_PANELS, raw.shape), raw, 0.0)
                down_part[s, rows_of(r), :] = raw - dot(left[s, rows_of(r), :], beside)
                return carry

            lax.fori_loop(0, rb, one, 0)

        def assemble(r, carry):
            tile = front[rows_of(r), 0:BLOCK]
            for s in range(leaves if has_c else 0):
                tile = tile + chosen(known[s], 0, r, rb, lambda t: down_part[s, block_slice(t), :])
            prow[rows_of(r), :] = tile
            return carry

        lax.fori_loop(0, rb, assemble, 0)

    @pl.when(top)
    def _():
        for s in range(leaves if has_c else 0):
            if s == 0:
                beside = chosen(table, 0, 0, rb, lambda t: left[0, block_slice(t), :])
            else:
                beside = left[s, third, :]
                beside = jnp.where(is_at(known[s], 0, 0, CHILD_PANELS, beside.shape), beside, 0.0)

            def one(c, carry, s=s, beside=beside):
                if s == 0:
                    raw = chosen(table, 0, 0, rb, lambda t: own[block_slice(t), rows_of(c)])
                else:
                    raw = other[s - 1, third, rows_of(c)]
                    raw = jnp.where(is_at(known[s], 0, 0, CHILD_PANELS, raw.shape), raw, 0.0)
                across[s, :, rows_of(c)] = raw - dot(beside, right[s, :, rows_of(c)])
                return carry

            lax.fori_loop(0, cb, one, 0)

        def assemble(c, carry):
            tile = front[0:BLOCK, rows_of(c)]
            for s in range(leaves if has_c else 0):
                tile = tile + chosen(known[s], 1, c, cb, lambda t: across[s, :, block_slice(t)])
            pcol[:, rows_of(c)] = tile
            return carry

        lax.fori_loop(0, cb, assemble, 0)

    @pl.when(corner)
    def _():
        ppiv[...] = prow[0:BLOCK, :]

    for b in range(1, frows):
        start(corner, ppiv, ppiv, sem("pp"), {"frow": b})
    for c in range(1, fcols):
        start(corner, ppiv, ppiv, sem("pp"), {"fcol": c})
    for q in range(CHUNKS):
        start(top, chunk(pcol, q, CHUNKS), chunk(pcol, q, CHUNKS), sem("pc", q), up)
    for c in range(1, fcols):
        start(first, prow, prow, sem("pr"), {"fcol": c})
    arrived(first & (i > 0), ppiv, sem("pp"), down)
    for c in range(1, fcols):
        start(first & (i > 0), ppiv, ppiv, sem("pp"), {"fcol": c})

    for s in range(1, leaves):
        high[...], low[...] = split(right[s])

        def corr_row(r, carry, s=s):
            corr[s - 1, rows_of(r), :] = dot_split(left[s, rows_of(r), :], high[...], low[...])
            return carry

        lax.fori_loop(0, rb, corr_row, 0)

    arrived(j > 0, ppiv, sem("pp"), root_row)
    turn = []

    def pass_parent():
        n = len(turn)
        turn.append(n)
        part = chunk(pcol, n, CHUNKS)
        arrived(inner_rows, part, sem("pc", n), down)
        start(inner_rows, part, part, sem("pc", n), up)

    upper, inverse = factor_block(ppiv[...], pass_parent)
    kp[...] = upper.T
    for q in range(CHUNKS):
        arrived(i == frows - 1, chunk(pcol, q, CHUNKS), sem("pc", q), down)
    arrived(j > 0, prow, sem("pr"), root_row)
    lprow[...] = dot_t(prow[...], inverse)
    lpcol[...] = dot(inverse, pcol[...])
    high[0:BLOCK, :], low[0:BLOCK, :] = split(lpcol[...])

    def parent_row(r, carry):
        value = front[rows_of(r), :] - dot_split(lprow[rows_of(r), :], high[0:BLOCK, :], low[0:BLOCK, :])
        update[rows_of(r), :] = jnp.where(top & (r == 0), 0.0, value)
        return carry

    lax.fori_loop(0, rb, parent_row, 0)

    @pl.when(first)
    def _():
        update[:, 0:BLOCK] = lprow[...]

    @pl.when(corner)
    def _():
        update[0:BLOCK, 0:BLOCK] = kp[...]

    update_copy = pltpu.make_async_copy(update, update_hbm, local_sem.at[2])
    update_copy.start()
    wait_pieces([0], inside)
    wait_pieces([1], inside)
    wait_pieces(panel, inside)
    wait_pieces(middle, inside)
    wait_pieces(last)

    for cond, copy in pending:
        pl.when(cond)(copy.wait_send)

    def subtract(r, carry):
        for s in range(1, leaves):
            other[s - 1, rows_of(r), :] = other[s - 1, rows_of(r), :] - corr[s - 1, rows_of(r), :]
        return carry

    lax.fori_loop(0, rb, subtract, 0)
    child_copy.wait()
    update_copy.wait()


def assemble_kernel(children, sources, where_am_i, update, *refs):
    blocks, same, out, child = refs[:children], *refs[children:]
    child[...] = same[...]
    r = pl.program_id(0)
    for c in range(out.shape[1] // BLOCK):
        span = slice(c * BLOCK, (c + 1) * BLOCK)
        tile = update[:, span]
        panel = (where_am_i[0] + r == 0) | ((where_am_i[1] == 0) & (c == 0))
        for s in range(children):
            source = sources[s, 1, c]
            keep = (sources[s, 0, r] >= 0) & (source >= 0) & jnp.logical_not(panel)
            at = pl.ds(pl.multiple_of(jnp.maximum(source, 0) * BLOCK, BLOCK), BLOCK)
            tile = tile + jnp.where(keep, blocks[s][:, at], 0.0)
        out[:, span] = tile


def assemble(sources, where_am_i, update, blocks):
    height, breadth = update.shape
    children = len(blocks)

    def moved(s):
        return lambda r, sources, where_am_i: (jnp.maximum(sources[s, 0, r], 0), 0)

    row = pl.BlockSpec((BLOCK, breadth), lambda r, sources, where_am_i: (r, 0))
    return pl.pallas_call(
        functools.partial(assemble_kernel, children),
        grid_spec=pltpu.PrefetchScalarGridSpec(
            num_scalar_prefetch=2,
            grid=(height // BLOCK,),
            in_specs=[row] + [pl.BlockSpec((BLOCK, breadth), moved(s)) for s in range(children)] + [row],
            out_specs=(row, row),
        ),
        out_shape=(jax.ShapeDtypeStruct((height, breadth), jnp.float32),) * 2,
        name="assemble",
    )(sources, where_am_i, update, *blocks, blocks[0])


def per_device(sizes, child_fronts, parent_front, block_maps):
    leaves, frows, fcols = sizes
    height, breadth = parent_front.shape
    assert fcols % leaves == 0 and fcols % 2 == 0
    rb, cb = height // BLOCK, breadth // BLOCK
    i, j = lax.axis_index("frow"), lax.axis_index("fcol")
    number = jnp.arange(block_maps.shape[1], dtype=jnp.int32)
    matches = block_maps[0][:, None] == number[None, :]
    inverse = jnp.sum(jnp.where(matches, number[:, None], 0), axis=0)
    deep = -(-max(rb, cb) // 8) * 8
    own_lines, sent_lines = [], []
    for count, position in ((rb, i), (cb, j)):
        source = lax.dynamic_slice_in_dim(inverse, position * count, count)
        kept = source >= CHILD_PANELS
        source = source - position * count
        to = jnp.maximum(inverse[0], CHILD_PANELS)
        swapped = jnp.where(source == to, CHILD_PANELS, jnp.where(source == CHILD_PANELS, to, source))
        swap = (position == 0) & (min(rb, cb) > CHILD_PANELS)
        swapped = jnp.where(swap, swapped, source)
        for lines, values in ((own_lines, source), (sent_lines, swapped)):
            lines.append(jnp.pad(jnp.where(kept, values, -1), (0, deep - count)))
    table, table_send = (
        jnp.broadcast_to(jnp.stack(lines)[:, :, None], (2, deep, BLOCK)) for lines in (own_lines, sent_lines)
    )
    f32 = jnp.float32
    block = jax.ShapeDtypeStruct((height, breadth), f32)
    vmem, away = pl.BlockSpec(memory_space=pltpu.VMEM), pl.BlockSpec(memory_space=pl.ANY)
    sends = (
        leaves * (frows - 1) + 2 * fcols + leaves * CHUNKS * 2 + leaves * fcols + leaves * 7
        + frows + fcols * 3 + 4 + fcols * leaves
    )
    square = (BLOCK, BLOCK)
    scratch = [
        pltpu.VMEM((height, breadth), f32),
        pltpu.VMEM((leaves, WIDE, WIDE), f32),
        pltpu.VMEM((WIDE, WIDE), f32),
        pltpu.VMEM((leaves, height, WIDE), f32),
        pltpu.VMEM((leaves, WIDE, breadth), f32),
        pltpu.VMEM((leaves, height, WIDE), f32),
        pltpu.VMEM((leaves, WIDE, breadth), f32),
        pltpu.VMEM((leaves - 1, height, breadth), f32),
        pltpu.VMEM((WIDE, WIDE), f32),
        pltpu.VMEM((leaves, WIDE, WIDE), f32),
        pltpu.VMEM((height, BLOCK), f32),
        pltpu.VMEM((BLOCK, breadth), f32),
        pltpu.VMEM(square, f32),
        pltpu.VMEM((leaves, height, BLOCK), f32),
        pltpu.VMEM((leaves, BLOCK, breadth), f32),
        pltpu.VMEM(square, f32),
        pltpu.VMEM((height, BLOCK), f32),
        pltpu.VMEM((BLOCK, breadth), f32),
        pltpu.VMEM((height, breadth), f32),
        pltpu.VMEM((height, breadth), f32),
        pltpu.VMEM((height, breadth), f32),
        pltpu.VMEM((WIDE, breadth), jnp.bfloat16),
        pltpu.VMEM((WIDE, breadth), jnp.bfloat16),
        pltpu.SemaphoreType.DMA((sends,)),
        pltpu.SemaphoreType.DMA((leaves * 14 + 10,)),
        pltpu.SemaphoreType.DMA((3,)),
    ]
    child, other, update, tables = pl.pallas_call(
        functools.partial(kernel, sizes),
        out_shape=(
            block,
            jax.ShapeDtypeStruct((leaves - 1, height, breadth), f32),
            block,
            jax.ShapeDtypeStruct((leaves - 1, 2, deep, BLOCK), jnp.int32),
        ),
        in_specs=[vmem] * 3 + [away],
        out_specs=(away, vmem, away, vmem),
        scratch_shapes=scratch,
        compiler_params=pltpu.CompilerParams(
            collective_id=0, has_side_effects=True, vmem_limit_bytes=56 * 2**20
        ),
        name="fronts",
    )(table, table_send, child_fronts[0], parent_front)
    sources = jnp.concatenate([table[None], tables], axis=0)[:, :, :, 0]
    where_am_i = jnp.stack([i, j]).astype(jnp.int32)
    parent, child = assemble(sources, where_am_i, update, [child] + [other[s] for s in range(leaves - 1)])
    return child[None], parent


def solution(mesh):
    sizes = (mesh.shape["leaf"], mesh.shape["frow"], mesh.shape["fcol"])
    return jax.shard_map(
        functools.partial(per_device, sizes),
        mesh=mesh,
        in_specs=(P("leaf", "frow", "fcol"), P("frow", "fcol"), P("leaf", None)),
        out_specs=(P("leaf", "frow", "fcol"), P("frow", "fcol")),
        check_vma=False,
    )
```

```python
import functools

import jax
import jax.numpy as jnp
from jax import lax
from jax.experimental import pallas as pl
from jax.experimental.pallas import tpu as pltpu
from jax.sharding import PartitionSpec as P

BLOCK = 128
CHILD_PANELS = 2
WIDE = BLOCK * CHILD_PANELS
CHUNKS = 4
MESH = pl.DeviceIdType.MESH


def dot(a, b, contract=((1,), (0,))):
    return lax.dot_general(
        a, b, (contract, ((), ())),
        precision=lax.Precision.HIGHEST, preferred_element_type=jnp.float32,
    )


def dot_t(a, b):
    return dot(a, b, ((1,), (1,)))


def split(x):
    high = x.astype(jnp.bfloat16)
    return high, (x - high.astype(jnp.float32)).astype(jnp.bfloat16)


def dot_split(a, high, low):
    a_high, a_low = split(a)

    def one(x, y):
        return lax.dot_general(x, y, (((1,), (0,)), ((), ())), preferred_element_type=jnp.float32)

    return one(a_high, high) + (one(a_high, low) + one(a_low, high))


def factor_block(block, between):
    shape = (BLOCK, BLOCK)
    row = lax.broadcasted_iota(jnp.int32, shape, 0)
    lane = lax.broadcasted_iota(jnp.int32, shape, 1)

    def turn(g, carry):
        m, v = carry
        active = row < BLOCK - 8 * g
        for t in range(8):
            scale = 1.0 / m[t : t + 1, t : t + 1]
            column = jnp.where(active & (row > t), jnp.broadcast_to(m[:, t : t + 1], shape), 0.0)
            pivot_m = m[t : t + 1, :] * scale
            pivot_v = v[t : t + 1, :] * scale
            m = m - column * pivot_m
            v = v - column * pivot_v
        m = pltpu.roll(m, BLOCK - 8, 1)
        m = jnp.concatenate([m[8:], m[:8]], axis=0)
        v = jnp.concatenate([v[8:], v[:8]], axis=0)
        return m, v

    carry = (block, jnp.where(row == lane, 1.0, 0.0))
    turns = BLOCK // 8 // CHUNKS
    for q in range(CHUNKS):
        carry = lax.fori_loop(q * turns, (q + 1) * turns, turn, carry)
        between()
    m, v = carry
    root = 1.0 / jnp.sqrt(jnp.sum(jnp.where(row == lane, m, 0.0), axis=1, keepdims=True))
    return jnp.where(lane >= row, m * root, 0.0), v * root


def kernel(sizes, table, table_send, own, front_hbm, child_hbm, other, update_hbm, tables,
           stage, dbuf, piv, rows, cols, left, right, corr, kbuf, wbuf,
           prow, pcol, ppiv, down_part, across, kp, lprow, lpcol, front, child, update, high, low, send_sem, recv_sem, local_sem):
    leaves, frows, fcols = sizes
    height, breadth = own.shape
    rb, cb = height // BLOCK, breadth // BLOCK
    has_c = rb > CHILD_PANELS and cb > CHILD_PANELS
    l, i, j = lax.axis_index("leaf"), lax.axis_index("frow"), lax.axis_index("fcol")
    top, first = i == 0, j == 0
    corner = top & first
    pending = []
    names = {}

    def sem(*name):
        return recv_sem.at[names.setdefault(name, len(names))]

    def start(cond, src, dst, signal, where):
        copy = pltpu.make_async_remote_copy(
            src_ref=src, dst_ref=dst, send_sem=send_sem.at[len(pending)], recv_sem=signal,
            device_id=where, device_id_type=MESH,
        )
        pending.append((cond, copy))
        pl.when(cond)(copy.start)

    def arrived(cond, dst, signal, where):
        copy = pltpu.make_async_remote_copy(
            src_ref=dst, dst_ref=dst, send_sem=send_sem.at[0], recv_sem=signal,
            device_id=where, device_id_type=MESH,
        )
        pl.when(cond)(copy.wait_recv)

    always = i >= 0
    up = {"frow": lax.rem(i + 1, frows)}
    down = {"frow": lax.rem(i + frows - 1, frows)}
    root_row = {"fcol": lax.rem(j + 1, fcols)}

    def leaf_at(s):
        return {"leaf": lax.rem(l + s, leaves)}

    def rows_of(k):
        return pl.ds(pl.multiple_of(k * BLOCK, BLOCK), BLOCK)

    def chunk(ref, q, count):
        size = ref.shape[0] // count
        return ref.at[pl.ds(q * size, size)]

    load = pltpu.make_async_copy(front_hbm, front, local_sem.at[0])
    load.start()

    barrier = pltpu.get_barrier_semaphore()
    for d in range(1, leaves):
        pl.semaphore_signal(barrier, inc=1, device_id=leaf_at(d), device_id_type=MESH)
    for d in range(1, frows):
        pl.semaphore_signal(barrier, inc=1, device_id={"frow": lax.rem(i + d, frows)}, device_id_type=MESH)
    for d in range(1, fcols):
        pl.semaphore_signal(barrier, inc=1, device_id={"fcol": lax.rem(j + d, fcols)}, device_id_type=MESH)
    pl.semaphore_wait(barrier, leaves + frows + fcols - 3)

    pivot_own = own.at[pl.ds(0, WIDE), pl.ds(0, WIDE)]

    def pivot_of(s):
        return pivot_own if s == 0 else other.at[s - 1, pl.ds(0, WIDE), pl.ds(0, WIDE)]

    def send_pivot(s):
        for b in range(1, frows):
            start(corner, pivot_of(s), dbuf.at[s], sem("d", s), {"frow": b})
        for c in range(1, fcols):
            if c % leaves == s:
                start(corner, pivot_of(s), piv, sem("piv"), {"fcol": c})

    def pass_pivot(s):
        inner = first & (i > 0)
        arrived(inner, dbuf.at[s], sem("d", s), down)
        for c in range(1, fcols):
            if c % leaves == s:
                start(inner, dbuf.at[s], piv, sem("piv"), {"fcol": c})

    send_pivot(0)
    for q in range(CHUNKS):
        start(top, chunk(own.at[pl.ds(0, WIDE)], q, CHUNKS), chunk(cols.at[0], q, CHUNKS), sem("c", 0, q), up)
    half = height // 2

    def send_rows(s, source):
        for c in range(1, fcols):
            if c == 1:
                start(first, source, rows.at[s], sem("r", s), {"fcol": c})
            else:
                part = pl.ds(c % 2 * half, half)
                start(first, source.at[part], rows.at[s, part], sem("r", s), {"fcol": c})

    def take_rows(s):
        partner = {"fcol": j + 1 - 2 * lax.rem(j, 2)}
        mine = rows.at[s, pl.ds(pl.multiple_of(lax.rem(j, 2) * half, 8), half)]
        theirs = rows.at[s, pl.ds(pl.multiple_of((1 - lax.rem(j, 2)) * half, 8), half)]
        arrived(j == 1, rows.at[s], sem("r", s), root_row)
        arrived(j > 1, mine, sem("r", s), root_row)
        start(j > 1, mine, mine, sem("r2", s), partner)
        arrived(j > 1, theirs, sem("r2", s), partner)

    send_rows(0, own.at[:, pl.ds(0, WIDE)])

    def is_at(ref, kind, k, t, shape):
        return jnp.broadcast_to(ref[kind, pl.ds(k, 1), 0:1], shape) == t

    def chosen(ref, kind, k, count, block):
        total = 0.0
        for t in range(count):
            part = block(t)
            total = total + jnp.where(is_at(ref, kind, k, t, part.shape), part, 0.0)
        return total

    def stage_rows(r, carry):
        stage[rows_of(r), :] = own[rows_of(r), :]
        return carry

    def block_slice(t):
        return slice(t * BLOCK, (t + 1) * BLOCK)

    def stage_cols(r, carry):
        held = stage[rows_of(r), block_slice(CHILD_PANELS)]
        value = held
        for t in range(CHILD_PANELS + 1, cb):
            here = stage[rows_of(r), block_slice(t)]
            match = is_at(table, 1, 0, t, here.shape)
            value = jnp.where(match, here, value)
            stage[rows_of(r), block_slice(t)] = jnp.where(match, held, here)
        stage[rows_of(r), block_slice(CHILD_PANELS)] = value
        return carry

    three = WIDE + BLOCK
    pieces = [(0, WIDE, 0, WIDE), (0, WIDE, WIDE, breadth)]
    if height > WIDE:
        pieces += [(WIDE, height, 0, WIDE), (WIDE, three, WIDE, breadth)]
    if height > three:
        pieces += [(three, height, WIDE, three), (three, height, three, breadth)]
    panel, middle, last = [2], [3, 4], [5]
    panel, middle, last = ([n for n in some if n < len(pieces)] for some in (panel, middle, last))

    def piece(ref, n):
        a, b, c, d = pieces[n]
        return ref.at[pl.ds(a, b - a), pl.ds(c, d - c)]

    def send_pieces(numbers, cond=always, source=stage):
        for n in numbers:
            for s in range(1, leaves):
                start(cond, piece(source, n), piece(other.at[s - 1], n), sem("y", s, n), leaf_at(s))

    def wait_pieces(numbers, cond=always):
        for n in numbers:
            for s in range(1, leaves):
                arrived(cond, piece(other.at[s - 1], n), sem("y", s, n), leaf_at(leaves - s))

    for s in range(1, leaves):
        start(always, table_send, tables.at[s - 1], sem("tables", s), leaf_at(s))
    send_pieces([0], source=own)
    send_pieces(panel, i > 0, own)
    lax.fori_loop(0, CHILD_PANELS, stage_rows, 0)
    if has_c:
        @pl.when(first)
        def _():
            lax.fori_loop(0, CHILD_PANELS, stage_cols, 0)
    send_pieces([1], top)
    lax.fori_loop(CHILD_PANELS, rb, stage_rows, 0)
    if has_c:
        @pl.when(top)
        def _():
            def fix(c, carry):
                held = own[block_slice(CHILD_PANELS), rows_of(c)]
                value = held
                for t in range(CHILD_PANELS + 1, rb):
                    here = own[block_slice(t), rows_of(c)]
                    match = is_at(table, 0, 0, t, here.shape)
                    value = jnp.where(match, here, value)
                    stage[block_slice(t), rows_of(c)] = jnp.where(match, held, here)
                stage[block_slice(CHILD_PANELS), rows_of(c)] = value
                return carry

            lax.fori_loop(0, cb, fix, 0)

        @pl.when(first)
        def _():
            lax.fori_loop(CHILD_PANELS, rb, stage_cols, 0)
    send_pieces(panel, top)
    send_pieces(middle[1:], i > 0)
    send_pieces([1], i > 0)
    send_pieces(middle, top)
    send_pieces(middle[:1], i > 0)

    @pl.when(top)
    def _():
        cols[0] = own[0:WIDE, :]

    @pl.when(first)
    def _():
        rows[0] = own[:, 0:WIDE]

    pass_pivot(0)

    @pl.when(corner)
    def _():
        piv[...] = own[0:WIDE, 0:WIDE]

    @pl.when(first & (i > 0))
    def _():
        piv[...] = dbuf[0]

    inner_rows = (i > 0) & (i < frows - 1)

    def pass_cols(s, q):
        here = chunk(cols.at[s], q, CHUNKS)
        arrived(inner_rows, here, sem("c", s, q), down)
        start(inner_rows, here, here, sem("c", s, q), up)

    edge = top | first
    inside = (i > 0) & (j > 0)
    wait_pieces([0], edge)
    for s in range(1, leaves):
        send_pivot(s)
    for s in range(1, leaves):
        pass_pivot(s)

    arrived(j > 0, piv, sem("piv"), root_row)
    slot = lax.rem(j, leaves)
    base = j - slot
    step = []

    def between():
        n = len(step)
        step.append(n)
        q = n % CHUNKS
        if n < CHUNKS:
            pass_cols(0, q)
        else:
            for s in range(1, leaves):
                pass_cols(s, q)
        if n == CHUNKS - 1:
            wait_pieces([1], top)
            for s in range(1, leaves):
                for p in range(CHUNKS):
                    source = chunk(other.at[s - 1, pl.ds(0, WIDE)], p, CHUNKS)
                    start(top, source, chunk(cols.at[s], p, CHUNKS), sem("c", s, p), up)

                @pl.when(top)
                def _(s=s):
                    cols[s] = other[s - 1, 0:WIDE, :]
        if n == CHUNKS + 1:
            send_pieces(last)
            wait_pieces(panel, first)
            for s in range(1, leaves):
                send_rows(s, other.at[s - 1, :, pl.ds(0, WIDE)])

                @pl.when(first)
                def _(s=s):
                    rows[s] = other[s - 1, :, 0:WIDE]

    lo, hi = slice(0, BLOCK), slice(BLOCK, WIDE)
    upper, inverse = factor_block(piv[lo, lo], between)
    kbuf[...] = jnp.zeros_like(kbuf)
    kbuf[lo, lo] = upper.T
    wbuf[slot, lo, lo] = inverse
    wbuf[slot, lo, hi] = jnp.zeros((BLOCK, BLOCK), jnp.float32)
    below = dot_t(piv[hi, lo], inverse)
    kbuf[hi, lo] = below
    upper, second = factor_block(piv[hi, hi] - dot_t(below, below), between)
    kbuf[hi, hi] = upper.T
    wbuf[slot, hi, hi] = second
    wbuf[slot, hi, lo] = -dot(second, dot(below, inverse))
    w_sems = [sem("w", s) for s in range(leaves)]
    w_first = names[("w", 0)]
    for d in range(1, leaves):
        start(always, wbuf.at[slot], wbuf.at[slot], recv_sem.at[w_first + slot], {"fcol": base + lax.rem(slot + d, leaves)})
    for d in range(1, leaves):
        from_slot = lax.rem(slot + d, leaves)
        arrived(always, wbuf.at[from_slot], recv_sem.at[w_first + from_slot], {"fcol": base + from_slot})

    for s in range(1, leaves):
        arrived(always, tables.at[s - 1], sem("tables", s), leaf_at(leaves - s))

    def make_panels(s):
        take_rows(s)
        for q in range(CHUNKS):
            arrived(i == frows - 1, chunk(cols.at[s], q, CHUNKS), sem("c", s, q), down)

        def wide(k):
            return pl.ds(pl.multiple_of(k * WIDE, WIDE), WIDE)

        def one_row(r, carry):
            left[s, wide(r), :] = dot_t(rows[s, wide(r), :], wbuf[s])
            return carry

        def one_col(c, carry):
            right[s, :, wide(c)] = dot(wbuf[s], cols[s, :, wide(c)])
            return carry

        lax.fori_loop(0, height // WIDE, one_row, 0)
        lax.fori_loop(0, breadth // WIDE, one_col, 0)

    make_panels(0)
    high[...], low[...] = split(right[0])

    def child_row(r, carry):
        value = own[rows_of(r), :] - dot_split(left[0, rows_of(r), :], high[...], low[...])
        child[rows_of(r), :] = jnp.where(top & (r < CHILD_PANELS), 0.0, value)
        return carry

    lax.fori_loop(0, rb, child_row, 0)

    @pl.when(first)
    def _():
        child[:, 0:WIDE] = left[0]

    @pl.when(corner)
    def _():
        child[0:WIDE, 0:WIDE] = kbuf[...]

    child_copy = pltpu.make_async_copy(child, child_hbm, local_sem.at[1])
    child_copy.start()
    for s in range(1, leaves):
        make_panels(s)
    wait_pieces([1], first & (i > 0))
    wait_pieces(panel, top & (j > 0))
    wait_pieces(middle, edge)
    load.wait()

    third = block_slice(CHILD_PANELS)
    known = [table] + [tables.at[s - 1] for s in range(1, leaves)]

    @pl.when(first)
    def _():
        for s in range(leaves if has_c else 0):
            if s == 0:
                beside = chosen(table, 1, 0, cb, lambda t: right[0, :, block_slice(t)])
            else:
                beside = right[s, :, third]
                beside = jnp.where(is_at(known[s], 1, 0, CHILD_PANELS, beside.shape), beside, 0.0)

            def one(r, carry, s=s, beside=beside):
                if s == 0:
                    raw = chosen(table, 1, 0, cb, lambda t: own[rows_of(r), block_slice(t)])
                else:
                    raw = other[s - 1, rows_of(r), third]
                    raw = jnp.where(is_at(known[s], 1, 0, CHILD_PANELS, raw.shape), raw, 0.0)
                down_part[s, rows_of(r), :] = raw - dot(left[s, rows_of(r), :], beside)
                return carry

            lax.fori_loop(0, rb, one, 0)

        def assemble(r, carry):
            tile = front[rows_of(r), 0:BLOCK]
            for s in range(leaves if has_c else 0):
                tile = tile + chosen(known[s], 0, r, rb, lambda t: down_part[s, block_slice(t), :])
            prow[rows_of(r), :] = tile
            return carry

        lax.fori_loop(0, rb, assemble, 0)

    @pl.when(top)
    def _():
        for s in range(leaves if has_c else 0):
            if s == 0:
                beside = chosen(table, 0, 0, rb, lambda t: left[0, block_slice(t), :])
            else:
                beside = left[s, third, :]
                beside = jnp.where(is_at(known[s], 0, 0, CHILD_PANELS, beside.shape), beside, 0.0)

            def one(c, carry, s=s, beside=beside):
                if s == 0:
                    raw = chosen(table, 0, 0, rb, lambda t: own[block_slice(t), rows_of(c)])
                else:
                    raw = other[s - 1, third, rows_of(c)]
                    raw = jnp.where(is_at(known[s], 0, 0, CHILD_PANELS, raw.shape), raw, 0.0)
                across[s, :, rows_of(c)] = raw - dot(beside, right[s, :, rows_of(c)])
                return carry

            lax.fori_loop(0, cb, one, 0)

        def assemble(c, carry):
            tile = front[0:BLOCK, rows_of(c)]
            for s in range(leaves if has_c else 0):
                tile = tile + chosen(known[s], 1, c, cb, lambda t: across[s, :, block_slice(t)])
            pcol[:, rows_of(c)] = tile
            return carry

        lax.fori_loop(0, cb, assemble, 0)

    @pl.when(corner)
    def _():
        ppiv[...] = prow[0:BLOCK, :]

    for b in range(1, frows):
        start(corner, ppiv, ppiv, sem("pp"), {"frow": b})
    for c in range(1, fcols):
        start(corner, ppiv, ppiv, sem("pp"), {"fcol": c})
    for q in range(CHUNKS):
        start(top, chunk(pcol, q, CHUNKS), chunk(pcol, q, CHUNKS), sem("pc", q), up)
    for c in range(1, fcols):
        start(first, prow, prow, sem("pr"), {"fcol": c})
    arrived(first & (i > 0), ppiv, sem("pp"), down)
    for c in range(1, fcols):
        start(first & (i > 0), ppiv, ppiv, sem("pp"), {"fcol": c})

    for s in range(1, leaves):
        high[...], low[...] = split(right[s])

        def corr_row(r, carry, s=s):
            corr[s - 1, rows_of(r), :] = dot_split(left[s, rows_of(r), :], high[...], low[...])
            return carry

        lax.fori_loop(0, rb, corr_row, 0)

    arrived(j > 0, ppiv, sem("pp"), root_row)
    turn = []

    def pass_parent():
        n = len(turn)
        turn.append(n)
        part = chunk(pcol, n, CHUNKS)
        arrived(inner_rows, part, sem("pc", n), down)
        start(inner_rows, part, part, sem("pc", n), up)

    upper, inverse = factor_block(ppiv[...], pass_parent)
    kp[...] = upper.T
    for q in range(CHUNKS):
        arrived(i == frows - 1, chunk(pcol, q, CHUNKS), sem("pc", q), down)
    arrived(j > 0, prow, sem("pr"), root_row)
    lprow[...] = dot_t(prow[...], inverse)
    lpcol[...] = dot(inverse, pcol[...])
    high[0:BLOCK, :], low[0:BLOCK, :] = split(lpcol[...])

    def parent_row(r, carry):
        value = front[rows_of(r), :] - dot_split(lprow[rows_of(r), :], high[0:BLOCK, :], low[0:BLOCK, :])
        update[rows_of(r), :] = jnp.where(top & (r == 0), 0.0, value)
        return carry

    lax.fori_loop(0, rb, parent_row, 0)

    @pl.when(first)
    def _():
        update[:, 0:BLOCK] = lprow[...]

    @pl.when(corner)
    def _():
        update[0:BLOCK, 0:BLOCK] = kp[...]

    update_copy = pltpu.make_async_copy(update, update_hbm, local_sem.at[2])
    update_copy.start()
    wait_pieces([0], inside)
    wait_pieces([1], inside)
    wait_pieces(panel, inside)
    wait_pieces(middle, inside)
    wait_pieces(last)

    for cond, copy in pending:
        pl.when(cond)(copy.wait_send)

    def subtract(r, carry):
        for s in range(1, leaves):
            other[s - 1, rows_of(r), :] = other[s - 1, rows_of(r), :] - corr[s - 1, rows_of(r), :]
        return carry

    lax.fori_loop(0, rb, subtract, 0)
    child_copy.wait()
    update_copy.wait()


def assemble_kernel(children, sources, where_am_i, update, *refs):
    blocks, same, out, child = refs[:children], *refs[children:]
    child[...] = same[...]
    r = pl.program_id(0)
    for c in range(out.shape[1] // BLOCK):
        span = slice(c * BLOCK, (c + 1) * BLOCK)
        tile = update[:, span]
        panel = (where_am_i[0] + r == 0) | ((where_am_i[1] == 0) & (c == 0))
        for s in range(children):
            source = sources[s, 1, c]
            keep = (sources[s, 0, r] >= 0) & (source >= 0) & jnp.logical_not(panel)
            at = pl.ds(pl.multiple_of(jnp.maximum(source, 0) * BLOCK, BLOCK), BLOCK)
            tile = tile + jnp.where(keep, blocks[s][:, at], 0.0)
        out[:, span] = tile


def assemble(sources, where_am_i, update, blocks):
    height, breadth = update.shape
    children = len(blocks)

    def moved(s):
        return lambda r, sources, where_am_i: (jnp.maximum(sources[s, 0, r], 0), 0)

    row = pl.BlockSpec((BLOCK, breadth), lambda r, sources, where_am_i: (r, 0))
    return pl.pallas_call(
        functools.partial(assemble_kernel, children),
        grid_spec=pltpu.PrefetchScalarGridSpec(
            num_scalar_prefetch=2,
            grid=(height // BLOCK,),
            in_specs=[row] + [pl.BlockSpec((BLOCK, breadth), moved(s)) for s in range(children)] + [row],
            out_specs=(row, row),
        ),
        out_shape=(jax.ShapeDtypeStruct((height, breadth), jnp.float32),) * 2,
        name="assemble",
    )(sources, where_am_i, update, *blocks, blocks[0])


def per_device(sizes, child_fronts, parent_front, block_maps):
    leaves, frows, fcols = sizes
    height, breadth = parent_front.shape
    assert fcols % leaves == 0 and fcols % 2 == 0
    rb, cb = height // BLOCK, breadth // BLOCK
    i, j = lax.axis_index("frow"), lax.axis_index("fcol")
    number = jnp.arange(block_maps.shape[1], dtype=jnp.int32)
    matches = block_maps[0][:, None] == number[None, :]
    inverse = jnp.sum(jnp.where(matches, number[:, None], 0), axis=0)
    deep = -(-max(rb, cb) // 8) * 8
    own_lines, sent_lines = [], []
    for count, position in ((rb, i), (cb, j)):
        source = lax.dynamic_slice_in_dim(inverse, position * count, count)
        kept = source >= CHILD_PANELS
        source = source - position * count
        to = jnp.maximum(inverse[0], CHILD_PANELS)
        swapped = jnp.where(source == to, CHILD_PANELS, jnp.where(source == CHILD_PANELS, to, source))
        swap = (position == 0) & (min(rb, cb) > CHILD_PANELS)
        swapped = jnp.where(swap, swapped, source)
        for lines, values in ((own_lines, source), (sent_lines, swapped)):
            lines.append(jnp.pad(jnp.where(kept, values, -1), (0, deep - count)))
    table, table_send = (
        jnp.broadcast_to(jnp.stack(lines)[:, :, None], (2, deep, BLOCK)) for lines in (own_lines, sent_lines)
    )
    f32 = jnp.float32
    block = jax.ShapeDtypeStruct((height, breadth), f32)
    vmem, away = pl.BlockSpec(memory_space=pltpu.VMEM), pl.BlockSpec(memory_space=pl.ANY)
    sends = (
        leaves * (frows - 1) + 2 * fcols + leaves * CHUNKS * 2 + leaves * fcols + leaves * 7
        + frows + fcols * 3 + 4 + fcols * leaves
    )
    square = (BLOCK, BLOCK)
    scratch = [
        pltpu.VMEM((height, breadth), f32),
        pltpu.VMEM((leaves, WIDE, WIDE), f32),
        pltpu.VMEM((WIDE, WIDE), f32),
        pltpu.VMEM((leaves, height, WIDE), f32),
        pltpu.VMEM((leaves, WIDE, breadth), f32),
        pltpu.VMEM((leaves, height, WIDE), f32),
        pltpu.VMEM((leaves, WIDE, breadth), f32),
        pltpu.VMEM((leaves - 1, height, breadth), f32),
        pltpu.VMEM((WIDE, WIDE), f32),
        pltpu.VMEM((leaves, WIDE, WIDE), f32),
        pltpu.VMEM((height, BLOCK), f32),
        pltpu.VMEM((BLOCK, breadth), f32),
        pltpu.VMEM(square, f32),
        pltpu.VMEM((leaves, height, BLOCK), f32),
        pltpu.VMEM((leaves, BLOCK, breadth), f32),
        pltpu.VMEM(square, f32),
        pltpu.VMEM((height, BLOCK), f32),
        pltpu.VMEM((BLOCK, breadth), f32),
        pltpu.VMEM((height, breadth), f32),
        pltpu.VMEM((height, breadth), f32),
        pltpu.VMEM((height, breadth), f32),
        pltpu.VMEM((WIDE, breadth), jnp.bfloat16),
        pltpu.VMEM((WIDE, breadth), jnp.bfloat16),
        pltpu.SemaphoreType.DMA((sends,)),
        pltpu.SemaphoreType.DMA((leaves * 14 + 10,)),
        pltpu.SemaphoreType.DMA((3,)),
    ]
    child, other, update, tables = pl.pallas_call(
        functools.partial(kernel, sizes),
        out_shape=(
            block,
            jax.ShapeDtypeStruct((leaves - 1, height, breadth), f32),
            block,
            jax.ShapeDtypeStruct((leaves - 1, 2, deep, BLOCK), jnp.int32),
        ),
        in_specs=[vmem] * 3 + [away],
        out_specs=(away, vmem, away, vmem),
        scratch_shapes=scratch,
        compiler_params=pltpu.CompilerParams(
            collective_id=0, has_side_effects=True, vmem_limit_bytes=56 * 2**20
        ),
        name="fronts",
    )(table, table_send, child_fronts[0], parent_front)
    sources = jnp.concatenate([table[None], tables], axis=0)[:, :, :, 0]
    where_am_i = jnp.stack([i, j]).astype(jnp.int32)
    parent, child = assemble(sources, where_am_i, update, [child] + [other[s] for s in range(leaves - 1)])
    return child[None], parent


def solution(mesh):
    sizes = (mesh.shape["leaf"], mesh.shape["frow"], mesh.shape["fcol"])
    return jax.shard_map(
        functools.partial(per_device, sizes),
        mesh=mesh,
        in_specs=(P("leaf", "frow", "fcol"), P("frow", "fcol"), P("leaf", None)),
        out_specs=(P("leaf", "frow", "fcol"), P("frow", "fcol")),
        check_vma=False,
    )
```
